256 devices in a mesh: blk: 64 (over z, x, core), head: 4 (over y), sample: 1.
Axes of the slice: x: 4, y: 4, z: 8, core: 2. Of those that a mesh axis runs over, the one named last changes fastest.
Arguments:
- query_single: bfloat16 [1024, 384], P(('sample', 'blk')), may hold values from -6 to 6
- query_frames: float32 [12, 1024], P(None, ('sample', 'blk')), may hold values from -6 to 6, as said below
- query_chain: int32 [1024], P(('sample', 'blk')), may hold values from 0 to 23
- key_single: bfloat16 [12288, 384], P(('sample', 'blk')), may hold values from -6 to 6
- key_frames: float32 [12, 12288], P(None, ('sample', 'blk')), may hold values from -6 to 6, as said below
- key_chain: int32 [12288], P(('sample', 'blk')), may hold values from 0 to 23
- key_mask: int32 [12288], P(('sample', 'blk')), may hold values 0 or 1
- pair: bfloat16 [1024, 12288, 128], P(('sample', 'blk'), 'head'), may hold values from -1600 to 1600
- w_q: bfloat16 [384, 192], P(None, 'head'), may hold values from -0.3125 to 0.3125
- w_k: bfloat16 [384, 192], P(None, 'head'), may hold values from -0.3125 to 0.3125
- w_v: bfloat16 [384, 192], P(None, 'head'), may hold values from -0.3125 to 0.3125
- w_qp: bfloat16 [384, 144], P(None, 'head'), may hold values from -0.3125 to 0.3125
- w_kp: bfloat16 [384, 144], P(None, 'head'), may hold values from -0.3125 to 0.3125
- w_vp: bfloat16 [384, 288], P(None, 'head'), may hold values from -0.3125 to 0.3125
- w_bias: bfloat16 [128, 12], replicated, may hold values from -1 to 1
- head_weight: float32 [12], P('head'), may hold values from -1 to 2
- chain_bias: float32 [12], P('head'), may hold values from -2 to 2
- w_out: bfloat16 [2112, 384], replicated, may hold values from -0.25 to 0.25
- ln_gain: float32 [384], replicated, may hold values from 0.5 to 1.5
- w_frame: bfloat16 [384, 6], replicated, may hold values from -0.3125 to 0.3125
Outputs:
- single_out: bfloat16 [1024, 384], P(('sample', 'blk'))
- frames_out: float32 [12, 1024], P(None, ('sample', 'blk'))
The draws below stay inside these ranges and needn't reach their ends.
Inputs may be any that keep to these rules, and one draw needn't show every extreme that they name: `query_frames`: the first nine rows are each residue's rotation matrix row after row, orthonormal with determinant one; the last three are its translation. `key_frames`: the first nine rows are each residue's rotation matrix row after row, orthonormal with determinant one; the last three are its translation.
All inputs are finite; a program needn't handle non-finite values. No bound on the sum of `key_mask` on one device may be relied on, other than what follows from the above.
Results may differ from the reference program's by a relative error of at most 0.009.
Values may be sent and summed in bfloat16 or wider, within the bound.
A program may use at most 128 MiB of HBM per device.

```python
import math
import jax
import jax.numpy as jnp
from jax import lax

CS = 384
CZ = 128
HEADS = 12
HEAD_C = 16
QPTS = 4
VPTS = 8
Q = 1024
N = 12288
N_BLK = 64


def rotation_rows(quat):
    w, x, y, z = (quat[0], quat[1], quat[2], quat[3])
    return jnp.stack([1.0 - 2.0 * (y * y + z * z), 2.0 * (x * y - w * z), 2.0 * (x * z + w * y), 2.0 * (x * y + w * z), 1.0 - 2.0 * (x * x + z * z), 2.0 * (y * z - w * x), 2.0 * (x * z - w * y), 2.0 * (y * z + w * x), 1.0 - 2.0 * (x * x + y * y)], axis=0)


def unit_quat(key, count):
    quat = jax.random.normal(key, (4, count), jnp.float32)
    return quat / jnp.sqrt(jnp.sum(quat * quat, axis=0, keepdims=True))


def draw_query_frames(key, part):
    key = jax.random.fold_in(key, 3)
    first, second = jax.random.split(key)
    rotation = rotation_rows(unit_quat(first, Q))
    trans = jnp.clip(1.5 * jax.random.normal(second, (3, Q), jnp.float32), -6.0, 6.0)
    return jnp.concatenate([rotation, trans], axis=0)


def draw_key_frames(key, part):
    key = jax.random.fold_in(key, 7)
    first, second = jax.random.split(key)
    rotation = rotation_rows(unit_quat(first, N))
    trans = jnp.clip(1.5 * jax.random.normal(second, (3, N), jnp.float32), -6.0, 6.0)
    return jnp.concatenate([rotation, trans], axis=0)


def draw_pair(key, part):
    key = jax.random.fold_in(key, 11)
    first = jax.random.fold_in(key, 0)
    values = jnp.clip(jax.random.normal(first, (Q, N, CZ), jnp.float32), -6.0, 6.0)
    return values.astype(jnp.bfloat16)


def set_ends(drawn, own_key, smallest, top_value):
    longest = drawn.shape.index(max(drawn.shape))
    spots = []
    for shift in (0, 1):
        where = [jax.random.randint(jax.random.fold_in(own_key, axis), (), 0, length) for axis, length in enumerate(drawn.shape)]
        where[longest] = (where[longest] + shift) % drawn.shape[longest]
        spots.append(tuple(where))
    return drawn.at[spots[0]].set(smallest).at[spots[1]].set(top_value)


def block_levels(key, extent, pieces, smallest, top_value):
    factor_of, own = 1.0, jax.random.fold_in(key, 6)
    for position, parts in pieces:
        steps = jnp.exp(jax.random.uniform(jax.random.fold_in(own, position), (parts,), jnp.float32, smallest / len(pieces), top_value / len(pieces)))
        factor_of = factor_of * jnp.repeat(steps, extent[position] // parts).reshape([-1 if axis == position else 1 for axis in range(len(extent))])
    return factor_of


def gaussian(own_key, shape, scale, limit, cuts=(), dtype=jnp.bfloat16):
    gain = block_levels(own_key, shape, cuts, -0.22, 0.18) if cuts else 1.0
    array = jax.random.normal(own_key, shape, jnp.float32) * scale * gain
    return jnp.minimum(jnp.maximum(array, -limit), limit).astype(dtype)


def setup_inputs(seed: int = 0, part: int = 0) -> dict:
    seeds = jax.random.split(jax.random.key(seed), 21)
    own_keys = jax.random.split(jax.random.fold_in(seeds[20], part), 21)
    return {
        "query_single": gaussian(own_keys[0], (Q, CS), 1.0, 6.0, ((0, 64),)),
        "query_frames": draw_query_frames(jax.random.fold_in(jax.random.fold_in(seeds[20], part), 71), part),
        "query_chain": set_ends(jax.random.randint(own_keys[2], (Q,), 0, 24), jax.random.fold_in(own_keys[2], 1), 0, 23).astype(jnp.int32),
        "key_single": gaussian(own_keys[3], (N, CS), 1.0, 6.0, ((0, 64),)),
        "key_frames": draw_key_frames(jax.random.fold_in(jax.random.fold_in(seeds[20], part), 71), part),
        "key_chain": set_ends(jax.random.randint(own_keys[5], (N,), 0, 24), jax.random.fold_in(own_keys[5], 1), 0, 23).astype(jnp.int32),
        "key_mask": set_ends((jax.random.randint(own_keys[6], (N,), 0, 8) < 7).astype(jnp.int32), jax.random.fold_in(own_keys[6], 1), 0, 1),
        "pair": draw_pair(jax.random.fold_in(jax.random.fold_in(seeds[20], part), 71), part),
        "w_q": gaussian(seeds[8], (CS, HEADS * HEAD_C), CS ** -0.5, 0.3125, ((1, 4),)),
        "w_k": gaussian(seeds[9], (CS, HEADS * HEAD_C), CS ** -0.5, 0.3125, ((1, 4),)),
        "w_v": gaussian(seeds[10], (CS, HEADS * HEAD_C), CS ** -0.5, 0.3125, ((1, 4),)),
        "w_qp": gaussian(seeds[11], (CS, HEADS * 3 * QPTS), CS ** -0.5, 0.3125, ((1, 4),)),
        "w_kp": gaussian(seeds[12], (CS, HEADS * 3 * QPTS), CS ** -0.5, 0.3125, ((1, 4),)),
        "w_vp": gaussian(seeds[13], (CS, HEADS * 3 * VPTS), CS ** -0.5, 0.3125, ((1, 4),)),
        "w_bias": gaussian(seeds[14], (CZ, HEADS), (CZ // 4) ** -0.5, 1.0),
        "head_weight": jnp.clip(-1.0 + 3.0 * jax.random.uniform(seeds[15], (HEADS,), jnp.float32) ** block_levels(seeds[15], (HEADS,), ((0, 4),), -0.2, 0.2), -1.0, 2.0),
        "chain_bias": jnp.clip(jax.random.uniform(seeds[16], (HEADS,), jnp.float32, -2.0, 2.0) * block_levels(seeds[16], (HEADS,), ((0, 4),), -0.4, 0.0), -2.0, 2.0),
        "w_out": gaussian(seeds[17], (HEADS * (HEAD_C + CZ + 4 * VPTS), CS), (HEADS * (HEAD_C + CZ + 4 * VPTS) // 4) ** -0.5, 0.25),
        "ln_gain": jnp.clip(1.0 + 0.1 * jax.random.normal(seeds[18], (CS,), jnp.float32), 0.5, 1.5),
        "w_frame": gaussian(seeds[19], (CS, 6), CS ** -0.5, 0.3125),
    }


def quat_rotation(w, x, y, z):
    return [1.0 - 2.0 * (y * y + z * z), 2.0 * (x * y - w * z), 2.0 * (x * z + w * y), 2.0 * (x * y + w * z), 1.0 - 2.0 * (x * x + z * z), 2.0 * (y * z - w * x), 2.0 * (x * z - w * y), 2.0 * (y * z + w * x), 1.0 - 2.0 * (x * x + y * y)]

def global_points(single, weights, frames, points):
    rows = single.shape[0]
    local = jnp.dot(single, weights, preferred_element_type=jnp.float32).reshape(rows, HEADS, 3, points)
    rotation = frames[:9].T.reshape(rows, 3, 3)
    moved = jnp.einsum('rab,rhbp->rhap', rotation, local, precision=lax.Precision.HIGHEST)
    return moved + frames[9:12].T[:, None, :, None]

def reference(query_single, query_frames, query_chain, key_single, key_frames, key_chain, key_mask, pair, w_q, w_k, w_v, w_qp, w_kp, w_vp, w_bias, head_weight, chain_bias, w_out, ln_gain, w_frame):
    high = lax.Precision.HIGHEST
    feature = HEAD_C + CZ + 4 * VPTS
    weight_l = math.sqrt(1.0 / 3.0)
    weight_c = math.sqrt(2.0 / (9.0 * QPTS))
    coeff = jax.nn.softplus(head_weight) * weight_c / 2.0
    q_s = jnp.dot(query_single, w_q, preferred_element_type=jnp.float32).astype(jnp.bfloat16).reshape(Q, HEADS, HEAD_C)
    k_s = jnp.dot(key_single, w_k, preferred_element_type=jnp.float32).astype(jnp.bfloat16).reshape(N, HEADS, HEAD_C)
    v_s = jnp.dot(key_single, w_v, preferred_element_type=jnp.float32).astype(jnp.bfloat16).reshape(N, HEADS, HEAD_C)
    k_s = k_s.astype(jnp.float32)
    v_s = v_s.astype(jnp.float32)
    q_glob = global_points(query_single, w_qp, query_frames, QPTS)
    k_glob = lax.optimization_barrier(global_points(key_single, w_kp, key_frames, QPTS).astype(jnp.bfloat16)).astype(jnp.float32)
    v_glob = lax.optimization_barrier(global_points(key_single, w_vp, key_frames, VPTS).astype(jnp.bfloat16)).astype(jnp.float32)
    k_norm = lax.optimization_barrier(jnp.sum(k_glob * k_glob, axis=(2, 3)))
    rot_q = query_frames[:9].T.reshape(Q, 3, 3)
    trans_q = query_frames[9:12].T
    blocks = N_BLK
    rows = Q // blocks

    def one_block(items):
        q_blk, qg_blk, chain_blk, pair_blk, rot_blk, trans_blk = items
        bias = jnp.dot(pair_blk, w_bias, preferred_element_type=jnp.float32).astype(jnp.bfloat16)
        bias = lax.optimization_barrier(bias).astype(jnp.float32)
        scalar = jnp.einsum('qhc,khc->qkh', q_blk.astype(jnp.float32), k_s, precision=high) / math.sqrt(HEAD_C)
        cross = jnp.einsum('qhap,khap->qkh', qg_blk, k_glob, precision=high)
        q_norm = lax.optimization_barrier(jnp.sum(qg_blk * qg_blk, axis=(2, 3)))
        dist = q_norm[:, None, :] + k_norm[None, :, :] - 2.0 * cross
        same = (chain_blk[:, None] == key_chain[None, :]).astype(jnp.float32)
        logit = weight_l * (scalar + bias + same[:, :, None] * chain_bias[None, None, :] - coeff[None, None, :] * dist)
        logit = jnp.where(key_mask[None, :, None] == 1, logit, -1000000000.0)
        peak = lax.optimization_barrier(jnp.max(logit, axis=1, keepdims=True))
        expo = jnp.exp(logit - peak)
        attn = expo / lax.optimization_barrier(jnp.sum(expo, axis=1, keepdims=True))
        o_s = jnp.einsum('qkh,khc->qhc', attn, v_s, precision=high)
        o_g = jnp.einsum('qkh,khap->qhap', attn, v_glob, precision=high)
        attn_b = lax.optimization_barrier(attn.astype(jnp.bfloat16)).astype(jnp.float32)
        o_pair = jnp.einsum('qkh,qkc->qhc', attn_b, pair_blk.astype(jnp.float32), precision=high)
        shifted = o_g - trans_blk[:, None, :, None]
        o_loc = jnp.einsum('qba,qhbp->qhap', rot_blk, shifted, precision=high)
        o_norm = jnp.sqrt(lax.optimization_barrier(jnp.sum(o_loc * o_loc, axis=2)) + 1e-08)
        feats = jnp.concatenate([o_s, o_pair, o_loc.reshape(rows, HEADS, 3 * VPTS), o_norm], axis=2)
        feats = feats.astype(jnp.bfloat16).reshape(rows, HEADS * feature)
        return jnp.dot(feats, w_out, preferred_element_type=jnp.float32)
    update = lax.map(one_block, (q_s.reshape(blocks, rows, HEADS, HEAD_C), q_glob.reshape(blocks, rows, HEADS, 3, QPTS), query_chain.reshape(blocks, rows), pair.reshape(blocks, rows, N, CZ), rot_q.reshape(blocks, rows, 3, 3), trans_q.reshape(blocks, rows, 3))).reshape(Q, CS)
    mixed = query_single.astype(jnp.float32) + update
    mean = lax.optimization_barrier(jnp.mean(mixed, axis=1, keepdims=True))
    centered = mixed - mean
    var = lax.optimization_barrier(jnp.mean(centered * centered, axis=1, keepdims=True))
    single_out = (centered / jnp.sqrt(var + 1e-05) * ln_gain[None, :]).astype(jnp.bfloat16)
    shift = jnp.dot(single_out, w_frame, preferred_element_type=jnp.float32)
    length = jnp.sqrt(1.0 + shift[:, 0] ** 2 + shift[:, 1] ** 2 + shift[:, 2] ** 2)
    entries = quat_rotation(1.0 / length, shift[:, 0] / length, shift[:, 1] / length, shift[:, 2] / length)
    rot_u = jnp.stack(entries, axis=1).reshape(Q, 3, 3)
    rot_new = jnp.einsum('qab,qbc->qac', rot_q, rot_u, precision=high)
    trans_new = jnp.einsum('qab,qb->qa', rot_q, shift[:, 3:6], precision=high) + trans_q
    frames_out = jnp.concatenate([rot_new.reshape(Q, 9).T, trans_new.T], axis=0)
    return (single_out, frames_out)
```

```python
import math

import jax
import jax.numpy as jnp
from jax import lax
from jax.experimental import pallas as pl
from jax.experimental.pallas import tpu as pltpu
from jax.sharding import PartitionSpec as P

F32 = jnp.float32
BF16 = jnp.bfloat16
HIGH = lax.Precision.HIGHEST
MESH = pl.DeviceIdType.MESH

HEADS = 12
QPTS = 4
ROWS = 192
GROUPS = 8
GROUP = 24
CHUNKS = 8
KEYS = 384
WEIGHT_L = math.sqrt(1.0 / 3.0)
WEIGHT_C = math.sqrt(2.0 / (9.0 * QPTS))

Z_IN, LEFT_IN, RIGHT_IN, HALF_LEFT_IN, HALF_RIGHT_IN, CORE_IN = 0, 2, 4, 6, 8, 10
ROWS_IN, WEIGHTS_IN, PART_IN, UPDATE_IN, META = 18, 21, 24, 27, 30
Z_OUT, Z_BACK, RIGHT_OUT, LEFT_OUT, HALF_RIGHT_OUT, HALF_LEFT_OUT, CORE_OUT = 0, 2, 3, 5, 7, 9, 11
ROWS_OUT, WEIGHTS_OUT, PART_OUT, UPDATE_OUT, META_OUT = 19, 22, 25, 28, 31


def iota(shape, dim):
    return lax.broadcasted_iota(jnp.int32, shape, dim)


def by3(v):
    return (v * 171) >> 9


def by12(v):
    return (v * 171) >> 11


def by24(v):
    return (v * 2731) >> 16


def by48(v):
    return (v * 1366) >> 16


def by80(v):
    return (v * 820) >> 16


def by96(v):
    return (v * 683) >> 16


def ones_where(cond, dtype=BF16):
    return jnp.where(cond, 1.0, 0.0).astype(dtype)


def mm(lhs, rhs, precision=None):
    return lax.dot_general(
        lhs, rhs, (((1,), (0,)), ((), ())), precision=precision, preferred_element_type=F32
    )


def nt(lhs, rhs, precision=None):
    return lax.dot_general(
        lhs, rhs, (((1,), (1,)), ((), ())), precision=precision, preferred_element_type=F32
    )


def short(v):
    return v.astype(BF16).astype(F32)


def split2(v):
    first = short(v)
    return first, short(v - first)


def split3(v):
    first = short(v)
    second = short(v - first)
    return first, second, short(v - first - second)


def head16(head):
    owner = by3(head)
    return owner * 4 + head - owner * 3


def quat_rotation(w, x, y, z):
    return [
        1.0 - 2.0 * (y * y + z * z),
        2.0 * (x * y - w * z),
        2.0 * (x * z + w * y),
        2.0 * (x * y + w * z),
        1.0 - 2.0 * (x * x + z * z),
        2.0 * (y * z - w * x),
        2.0 * (x * z - w * y),
        2.0 * (y * z + w * x),
        1.0 - 2.0 * (x * x + y * y),
    ]


def own_rows(single, meta, w_q, w_k, w_qp, head_weight, chain_bias):
    rows = 48
    row = iota((rows, 1), 0)
    query = by3(row)
    local_head = row - query * 3
    spread = query == iota((rows, 16), 1)
    single_rows = mm(ones_where(spread), single).astype(BF16)
    q_s = mm(single_rows, w_q).astype(BF16).astype(F32)
    col = iota((rows, 48), 1)
    q_s = jnp.where((col >> 4) == local_head, q_s, 0.0).astype(BF16)
    scalar = nt(q_s, w_k) * (WEIGHT_L / 4.0)

    frames = nt(ones_where(spread, F32), meta, HIGH)
    local = mm(single_rows, w_qp)
    col = iota((rows, 36), 1)
    local = jnp.where(by12(col) == local_head, local, 0.0)
    lane = iota((1, 128), 1)
    comp = jnp.where(lane < 12, lane, lane - 12)
    axis = comp >> 2
    point = comp & 3
    inside = lane < 24
    source = iota((36, 128), 0)
    source = source - by12(source) * 12
    entry = iota((16, 128), 0)
    placed = mm(frames, ones_where((entry == axis + 9) & inside, F32), HIGH)
    for b in range(3):
        here = mm(local, ones_where((source == point + 4 * b) & inside, F32), HIGH)
        turn = mm(frames, ones_where((entry == axis * 3 + b) & inside, F32), HIGH)
        placed = placed + turn * here
    norm = jnp.sum(jnp.where(lane < 12, placed * placed, 0.0), axis=1, keepdims=True)

    def per_head(ref):
        return jnp.where(local_head == 0, ref[0], jnp.where(local_head == 1, ref[1], ref[2]))

    weight = per_head(head_weight)
    soft = jnp.maximum(weight, 0.0) + jnp.log(1.0 + jnp.exp(-jnp.abs(weight)))
    coeff = soft * (WEIGHT_L * WEIGHT_C / 2.0)
    point_hi, point_lo = split2(2.0 * coeff * placed)
    chain_hi, chain_lo = split2(per_head(chain_bias) * WEIGHT_L)
    own_chain = frames[:, 12:13]
    lane_f = lane.astype(F32)
    compact = jnp.where(lane < 12, point_hi, jnp.where(inside, point_lo, 0.0))
    compact = jnp.where((lane >= 24) & (lane < 48) & (own_chain == lane_f - 24.0), chain_hi, compact)
    compact = jnp.where((lane >= 48) & (lane < 72) & (own_chain == lane_f - 48.0), chain_lo, compact)
    for first, values in ((72, split3(-coeff * norm)), (75, split3(coeff))):
        for step, value in enumerate(values):
            compact = jnp.where(lane == first + step, value, compact)
    return scalar.astype(BF16), compact.astype(BF16)


def own_weights(w_kp, w_v, w_vp):
    row = iota((48, 36), 0)
    col = iota((48, 36), 1)
    head = row & 3
    pick = (col == head * 12 + (row >> 4) * 4 + ((row >> 2) & 3)) & (head < 3)
    key_points = nt(ones_where(pick), w_kp).astype(BF16)
    values = nt(ones_where(iota((48, 48), 0) == iota((48, 48), 1)), w_v).astype(BF16)
    row = iota((80, 72), 0)
    col = iota((80, 72), 1)
    b = by24(row)
    rest = row - b * 24
    pick = (col == (rest >> 3) * 24 + b * 8 + (rest & 7)) & (row < 72)
    value_points = nt(ones_where(pick), w_vp).astype(BF16)
    return key_points, values, value_points


def all_rows(packs):
    shape = (ROWS, ROWS)
    row, col = iota(shape, 0), iota(shape, 1)
    query = by12(row)
    owner = by48(col)
    rest = col - owner * 48
    col_query = by3(rest)
    pick = (query == col_query) & (row - query * 12 == owner * 3 + rest - col_query * 3)
    rows = mm(ones_where(pick), packs).astype(BF16)
    compact = rows[:, 384:]
    lane = iota((1, 512), 1)
    again = jnp.where(lane < 192, lane, lane - 192)
    source = ((again >> 6) * 4 + ((again >> 4) & 3)) + jnp.where(lane < 192, 0, 12)
    source = jnp.where(lane >= 384, -1, source)
    source = jnp.where((lane >= 384) & (lane < 408), lane - 360, source)
    source = jnp.where((lane >= 416) & (lane < 440), lane - 368, source)
    source = jnp.where((lane >= 496) & (lane < 499), lane - 424, source)
    other = mm(compact, ones_where(iota((128, 512), 0) == source))
    row = iota((ROWS, 1), 0)
    place = head16(row - by12(row) * 12)
    mine = (lane & 15) == place
    other = jnp.where(mine | (lane >= 384), other, 0.0)
    other = jnp.where(mine & (lane >= 448) & (lane < 496), 1.0, other)
    spot, col = iota((16, ROWS), 0), iota((16, ROWS), 1)
    pick = (head16(col) == spot) & (col < 12)
    factors = mm(ones_where(pick), compact)
    factor = factors[:, 75:76] + factors[:, 76:77] + factors[:, 77:78]
    return rows[:, :384], other.astype(BF16), factor


def kernel(
    single_q, meta_q, single_k, meta_k, pair, w_q, w_k, w_v, w_qp, w_kp, w_vp, w_bias, w_out, gain, w_frame,
    head_weight, chain_bias,
    single_out, frames_out,
    v_single, v_meta, v_wq, v_wk, v_wv, v_wqp, v_wkp, v_wvp, v_wbias, v_wout, v_gain, v_wframe,
    pairs, keys, metas, bias, pack_rows, pack_weights,
    rows_single, rows_other, w_points, w_values, w_vpoints, factors, bias_rows,
    acc_pair, acc_single, acc_points, top, total,
    part_out, part_in, updates,
    local_sem, pair_sem, send_sem, recv_sem,
):
    y = lax.axis_index("head")
    blk = lax.axis_index("blk")
    z = lax.div(blk, 8)
    core = lax.rem(blk, 2)
    x = lax.rem(lax.div(blk, 2), 4)
    r = lax.rem(z - 2 * y + 8, 8)
    upper = (r >= 1) & (r <= 4)
    depth = jnp.where(upper, r - 1, lax.rem(8 - r, 8))
    step_z = jnp.where(upper, 1, -1)
    near = jnp.where(upper, 1, 0)

    def device(zz, xx, cc):
        return (zz * 4 + xx) * 2 + cc

    out_z = device(lax.rem(z + step_z + 8, 8), x, core)
    in_z = device(lax.rem(z - step_z + 8, 8), x, core)
    right = device(z, lax.rem(x + 1, 4), core)
    left = device(z, lax.rem(x + 3, 4), core)
    sibling = device(z, x, 1 - core)

    small = [
        (single_q, v_single), (meta_q, v_meta), (w_q, v_wq), (w_k, v_wk), (w_qp, v_wqp), (w_kp, v_wkp),
        (w_v, v_wv), (w_vp, v_wvp), (w_bias, v_wbias), (gain, v_gain), (w_frame, v_wframe),
        (w_out.at[pl.ds(pl.multiple_of(y * 528, 528), 528)], v_wout),
    ]
    small = [pltpu.make_async_copy(src, dst, local_sem.at[i]) for i, (src, dst) in enumerate(small)]

    def item(i):
        phase = 0 if i in (0, 1, 2, 6) else 1
        kind = i if i < 3 else (i - 3 if i < 6 else 3)
        plane = near if phase == 0 else 1 - near
        return phase, kind, plane * 4 + lax.rem(x + (0, 3, 1, 2)[kind], 4)

    own_index = item(0)[2]
    own_copies = [
        pltpu.make_async_copy(single_k, keys.at[own_index, core], local_sem.at[12]),
        pltpu.make_async_copy(meta_k, metas.at[own_index, core], local_sem.at[13]),
    ]
    pair_copies = [
        pltpu.make_async_copy(pair.at[pl.ds(2 * g, 2)], pairs.at[pl.ds(2 * g, 2)], pair_sem.at[g])
        for g in range(GROUPS)
    ]

    barrier = pltpu.get_barrier_semaphore()
    for other in (
        device(lax.rem(z + 1, 8), x, core), device(lax.rem(z + 7, 8), x, core), right, left, sibling
    ):
        pl.semaphore_signal(barrier, inc=1, device_id={"blk": other}, device_id_type=MESH)
    for step in (1, 2, 3):
        pl.semaphore_signal(
            barrier, inc=1, device_id={"head": lax.rem(y + step, 4)}, device_id_type=MESH
        )

    @pl.when(depth == 0)
    def _():
        for copy in own_copies:
            copy.start()

    for copy in small:
        copy.start()
    for copy in pair_copies:
        copy.start()

    def remote(src, dst, sent, received, target):
        return pltpu.make_async_remote_copy(
            src_ref=src, dst_ref=dst, send_sem=send_sem.at[sent], recv_sem=recv_sem.at[received],
            device_id=target, device_id_type=MESH,
        )

    def block(index, cc, sent, received, target, part=None, meta=True):
        ref = keys.at[index, cc]
        if part is not None:
            ref = keys.at[index, cc, pl.ds(96 * part, 96)]
        copies = [remote(ref, ref, sent, received, {"blk": target})]
        if meta:
            ref = metas.at[index, cc]
            copies.append(remote(ref, ref, sent + META_OUT, received + META, {"blk": target}))
        return copies

    def sends(i):
        phase, kind, index = item(i)
        result = []
        if kind == 0:
            result.append((depth < 3, block(index, core, Z_OUT + phase, Z_IN + phase, out_z)))
            if phase == 0:
                result.append((depth == 0, block(index, core, Z_BACK, Z_IN + 1, in_z)))
            result.append((None, block(index, core, RIGHT_OUT + phase, LEFT_IN + phase, right)))
            result.append((None, block(index, core, LEFT_OUT + phase, RIGHT_IN + phase, left)))
        if kind == 1:
            result.append((None, block(index, core, HALF_RIGHT_OUT + phase, HALF_LEFT_IN + phase, right, 0)))
        if kind == 2:
            result.append(
                (None, block(index, core, HALF_LEFT_OUT + phase, HALF_RIGHT_IN + phase, left, 1, False))
            )
        result.append((None, block(index, core, CORE_OUT + i, CORE_IN + i, sibling)))
        return result

    def run(condition, copies, verb):
        def act():
            for copy in copies:
                getattr(copy, verb)()

        if condition is None:
            act()
        else:
            pl.when(condition)(act)

    def event(i):
        phase, kind, index = item(i)
        if kind == 0:
            arriving = block(index, core, 0, Z_IN + phase, sibling)
            run(depth > 0 if phase == 0 else None, arriving, "wait_recv")
        elif kind == 3:
            first = block(index, core, 0, HALF_LEFT_IN + phase, sibling, 0)
            second = block(index, core, 0, HALF_RIGHT_IN + phase, sibling, 1, False)
            for copy in first + second:
                copy.wait_recv()
        else:
            place = (LEFT_IN, RIGHT_IN)[kind - 1] + phase
            for copy in block(index, core, 0, place, sibling):
                copy.wait_recv()
        for condition, copies in sends(i):
            run(condition, copies, "start")

    def at(*by_depth):
        value = by_depth[3]
        for k in (2, 1, 0):
            value = jnp.where(depth == k, by_depth[k], value)
        return value

    slots = [
        at(-1, 4, 8, 8),
        at(4, 8, 8, 8),
        at(4, 8, 8, 9),
        at(4, 8, 8, 9),
        at(8, 9, 10, 10),
        at(8, 9, 10, 10),
        at(8, 9, 10, 11),
        at(10, 11, 11, 11),
    ]

    pl.semaphore_wait(barrier, 8)

    @pl.when(depth == 0)
    def _():
        for copy in own_copies:
            copy.wait()
        event(0)

    for copy in small:
        copy.wait()
    scalar, compact = own_rows(
        v_single[...], v_meta[...], v_wq[...], v_wk[...], v_wqp[...], head_weight, chain_bias
    )
    pack_rows[y, :, :384] = scalar
    pack_rows[y, :, 384:] = compact
    key_points, values, value_points = own_weights(v_wkp[...], v_wv[...], v_wvp[...])
    pack_weights[y, :48] = key_points
    pack_weights[y, 48:96] = values
    pack_weights[y, 96:] = value_points

    def exchange(src, dst, sent, received):
        out, arriving = [], []
        for step in (1, 2, 3):
            peer = lax.rem(y + step, 4)
            origin = lax.rem(y + 4 - step, 4)
            out.append(remote(src(peer), dst.at[y], sent + step - 1, received + step - 1, {"head": peer}))
            arriving.append(
                remote(dst.at[origin], dst.at[origin], sent + step - 1, received + step - 1, {"head": peer})
            )
        return out, arriving

    rows_sent, rows_arriving = exchange(lambda peer: pack_rows.at[y], pack_rows, ROWS_OUT, ROWS_IN)
    weights_sent, weights_arriving = exchange(
        lambda peer: pack_weights.at[y], pack_weights, WEIGHTS_OUT, WEIGHTS_IN
    )
    for copy in rows_sent + weights_sent:
        copy.start()

    row, col = iota((32, 128), 0), iota((32, 12), 1)
    pick_row = iota((32, 12), 0)
    first = nt(ones_where(pick_row == col), v_wbias[...])
    second = nt(ones_where(pick_row == col + 12), v_wbias[...])
    bias_rows[:, :128] = first.astype(BF16)
    bias_rows[:, 128:] = second.astype(BF16)

    def bias_step(t, _):
        pltpu.make_async_copy(pair.at[pl.ds(2 * t, 2)], pairs.at[pl.ds(2 * t, 2)], pair_sem.at[t]).wait()
        for c in range(0, CHUNKS, 2):
            block_a = pairs[2 * t, c : c + 2].reshape(2 * KEYS, 128)
            block_b = pairs[2 * t + 1, c : c + 2].reshape(2 * KEYS, 128)
            out = nt(bias_rows[...], jnp.concatenate([block_a, block_b], axis=1))[:GROUP]
            out = short(out) * WEIGHT_L
            bias[c, t] = out[:, :KEYS]
            bias[c + 1, t] = out[:, KEYS:]
        for i in range(6):
            pl.when(slots[i] == t)(lambda i=i: event(i))
        return 0

    lax.fori_loop(0, GROUPS, bias_step, 0)

    for copy in rows_arriving + weights_arriving:
        copy.wait_recv()
    for_single, for_other, factor = all_rows(pack_rows[...].reshape(ROWS, 512))
    rows_single[...] = for_single
    rows_other[...] = for_other
    factors[...] = -factor
    packs = pack_weights[...]
    row, col = iota((ROWS, ROWS), 0), iota((ROWS, ROWS), 1)
    place = row & 15
    pick = col == (place >> 2) * 48 + (row >> 6) * 16 + ((row >> 4) & 3) * 4 + (place & 3)
    w_points[...] = mm(ones_where(pick), packs[:, :48].reshape(ROWS, 384)).astype(BF16)
    w_values[...] = packs[:, 48:96].reshape(ROWS, 384)
    row, col = iota((288, 320), 0), iota((288, 320), 1)
    b = by96(row)
    rest = row - b * 96
    owner = by24(rest)
    pick = col == owner * 80 + b * 24 + rest - owner * 24
    w_vpoints[...] = mm(ones_where(pick), packs[:, 96:].reshape(320, 384)).astype(BF16)

    acc_pair[...] = jnp.zeros_like(acc_pair)
    acc_single[...] = jnp.zeros_like(acc_single)
    acc_points[...] = jnp.zeros_like(acc_points)
    top[...] = jnp.full_like(top, -1e30)
    total[...] = jnp.zeros_like(total)

    indices = [item(i)[2] for i in range(8)]

    def index_of(i):
        value = indices[7]
        for k in range(7):
            value = jnp.where(i == k, indices[k], value)
        return value

    def key_meta(index):
        half = iota((16, 128), 1) < 64
        first, second = metas[index, 0], metas[index, 1]
        start = pltpu.roll(second[:, :128], 64, 1)
        end = pltpu.roll(second[:, 128:], 64, 1)
        return [first[:, :128], jnp.where(half, first[:, 128:], start), jnp.where(half, start, end)]

    def key_step(s, _):
        for i in range(8):
            pl.when(slots[i] == s + 8)(lambda i=i: event(i))
        pair_of = []
        for k in range(2):
            i = 2 * s + k
            index = index_of(i)
            pair_of.append(index)
            here = keys.at[index, 1 - core]
            remote(here, here, 0, CORE_IN + i, {"blk": sibling}).wait_recv()
            here = metas.at[index, 1 - core]
            remote(here, here, 0, META + CORE_IN + i, {"blk": sibling}).wait_recv()

        single = jnp.concatenate([keys[index].reshape(KEYS, 384) for index in pair_of], axis=0)
        meta = jnp.concatenate(key_meta(pair_of[0]) + key_meta(pair_of[1]), axis=1)

        def placed(local, rows):
            result = []
            for a in range(3):
                moved = meta[9 + a : 10 + a] + meta[3 * a : 3 * a + 1] * local[:rows]
                moved = moved + meta[3 * a + 1 : 3 * a + 2] * local[rows : 2 * rows]
                moved = moved + meta[3 * a + 2 : 3 * a + 3] * local[2 * rows :]
                result.append(moved.astype(BF16))
            return result

        points = placed(nt(w_points[...], single), 64)
        square = 0.0
        for part in points:
            wide = part.astype(F32)
            square = square + wide * wide
        norm = square[:16] + square[16:32] + square[32:48] + square[48:]
        norms = [v.astype(BF16) for v in split3(norm * factors[...])]
        width = 2 * KEYS
        chains = ones_where(meta[12:13] == iota((32, width), 0).astype(F32))
        others = jnp.concatenate(
            points + points + [chains, chains] + norms + [jnp.full((16, width), 1.0, BF16)], axis=0
        )
        logit = nt(rows_single[...], single) + mm(rows_other[...], others)
        logit = logit + jnp.concatenate([bias[index].reshape(ROWS, KEYS) for index in pair_of], axis=1)
        logit = jnp.where(meta[13:14] > 0.5, logit, -1000000000.0)
        old = top[...]
        new = jnp.maximum(old, jnp.max(logit, axis=1, keepdims=True))
        scale = jnp.exp(old - new)
        weight = jnp.exp(logit - new)
        top[...] = new
        total[...] = total[...] * scale + jnp.sum(weight, axis=1, keepdims=True)
        weight_b = weight.astype(BF16)
        acc_single[...] = acc_single[...] * scale + mm(weight_b, single)
        vpoints = jnp.concatenate(placed(nt(w_vpoints[...], single), 96), axis=0)
        acc_points[...] = acc_points[...] * scale + nt(weight_b, vpoints)
        upper_rows = iota((GROUP, 128), 0) < 12
        for g in range(GROUPS):
            lo = g * GROUP
            there = jnp.concatenate(
                [
                    jnp.concatenate([pairs[2 * g, index] for index in pair_of], axis=0),
                    jnp.concatenate([pairs[2 * g + 1, index] for index in pair_of], axis=0),
                ],
                axis=1,
            )
            out = mm(weight[lo : lo + GROUP].astype(BF16), there)
            out = jnp.where(upper_rows, out[:, :128], out[:, 128:])
            acc_pair[g] = acc_pair[g] * scale[lo : lo + GROUP] + out
        return 0

    lax.fori_loop(0, 4, key_step, 0)

    inverse = 1.0 / total[...]
    row = iota((ROWS, 1), 0)
    head = row - by12(row) * 12
    pair_part = (acc_pair[...].reshape(ROWS, 128) * inverse).astype(BF16)
    hi, lo = split2(acc_single[...] * inverse)
    scalar = nt(hi.astype(BF16), w_values[...]) + nt(lo.astype(BF16), w_values[...])
    scalar = jnp.where((iota((ROWS, ROWS), 1) >> 4) == head, scalar, 0.0).astype(BF16)
    fold = ones_where((iota((ROWS, 128), 0) & 15) == iota((ROWS, 128), 1))
    other = mm(scalar, fold)
    col = iota((1, 288), 1)
    rest = col - by96(col) * 96
    hi, lo = split2(jnp.where((rest >> 3) == head, acc_points[...] * inverse, 0.0))
    source, lane = iota((288, 128), 0), iota((288, 128), 1)
    b = by96(source)
    target = b * 8 + (source & 7)
    other = other + mm(hi.astype(BF16), ones_where(lane == target + 16))
    other = other + mm(lo.astype(BF16), ones_where(lane == target + 40))
    lane = iota((1, 128), 1)
    for start, value in ((64, top[...]), (67, total[...])):
        for step, piece in enumerate(split3(value)):
            other = jnp.where(lane == start + step, piece, other)
    row, col = iota((ROWS, ROWS), 0), iota((ROWS, ROWS), 1)
    query = by12(col)
    pick = ones_where(((row & 15) == query) & ((row >> 4) == col - query * 12))
    moved = mm(pick, jnp.concatenate([pair_part, other.astype(BF16)], axis=1)).astype(BF16)
    part_out[...] = moved.reshape(4, 48, 256)

    parts_sent, parts_arriving = exchange(lambda peer: part_out.at[peer], part_in, PART_OUT, PART_IN)
    for copy in parts_sent:
        copy.start()
    part_in[y] = part_out[y]
    for copy in parts_arriving:
        copy.wait_recv()

    parts = [part_in[k].astype(F32) for k in range(4)]
    tops = [p[:, 192:193] + p[:, 193:194] + p[:, 194:195] for p in parts]
    best = jnp.maximum(jnp.maximum(tops[0], tops[1]), jnp.maximum(tops[2], tops[3]))
    shares = [
        (p[:, 195:196] + p[:, 196:197] + p[:, 197:198]) * jnp.exp(t - best) for p, t in zip(parts, tops)
    ]
    inverse = 1.0 / (shares[0] + shares[1] + shares[2] + shares[3])
    sums = sum(p * (s * inverse) for p, s in zip(parts, shares))
    o_pair = sums[:, :128].astype(BF16)
    other = sums[:, 128:]
    frames = nt(ones_where((iota((48, 16), 0) & 15) == iota((48, 16), 1), F32), v_meta[...], HIGH)
    lane = iota((1, 128), 1)
    inside = (lane >= 16) & (lane < 40)
    axis = (lane - 16) >> 3
    point = lane & 7
    source = iota((128, 128), 0)
    entry = iota((16, 128), 0)
    located = 0.0
    for b in range(3):
        pick = ((source == point + 16 + 8 * b) | (source == point + 40 + 8 * b)) & inside
        shifted = mm(other, ones_where(pick, F32), HIGH) - frames[:, 9 + b : 10 + b]
        turn = mm(frames, ones_where((entry == 3 * b + axis) & inside, F32), HIGH)
        located = located + turn * shifted
    square = located * located
    last = (lane >= 40) & (lane < 48)
    pick = (source >= 16) & (source < 40) & ((source & 7) == point) & last
    length = jnp.sqrt(mm(square, ones_where(pick, F32), HIGH) + 1e-08)
    feats = jnp.where(lane < 16, other, jnp.where(inside, located, jnp.where(last, length, 0.0)))
    feats = feats.astype(BF16)[:, :48]
    update = 0.0
    for k in range(3):
        here = slice(16 * k, 16 * k + 16)
        w = 176 * k
        update = update + mm(o_pair[here], v_wout[w + 16 : w + 144])
        rest = jnp.concatenate([v_wout[w : w + 16], v_wout[w + 144 : w + 176]], axis=0)
        update = update + mm(feats[here], rest)
    updates[y] = update
    updates_sent, updates_arriving = exchange(lambda peer: updates.at[y], updates, UPDATE_OUT, UPDATE_IN)
    for copy in updates_sent:
        copy.start()
    for copy in updates_arriving:
        copy.wait_recv()

    mixed = v_single[...].astype(F32) + updates[0] + updates[1] + updates[2] + updates[3]
    mean = jnp.mean(mixed, axis=1, keepdims=True)
    centered = mixed - mean
    var = jnp.mean(centered * centered, axis=1, keepdims=True)
    out = (centered / jnp.sqrt(var + 1e-05) * v_gain[...]).astype(BF16)
    single_out[...] = out
    w_rows = nt(ones_where(iota((16, 6), 0) == iota((16, 6), 1)), v_wframe[...]).astype(BF16)
    shift = nt(w_rows, out)
    u = [shift[k : k + 1] for k in range(6)]
    length = jnp.sqrt(1.0 + u[0] * u[0] + u[1] * u[1] + u[2] * u[2])
    turn = quat_rotation(1.0 / length, u[0] / length, u[1] / length, u[2] / length)
    rot = [v_meta[k : k + 1] for k in range(12)]
    for a in range(3):
        for c in range(3):
            k = 3 * a + c
            frames_out[k : k + 1] = (
                rot[3 * a] * turn[c] + rot[3 * a + 1] * turn[3 + c] + rot[3 * a + 2] * turn[6 + c]
            )
        moved = rot[3 * a] * u[3] + rot[3 * a + 1] * u[4] + rot[3 * a + 2] * u[5]
        frames_out[9 + a : 10 + a] = moved + rot[9 + a]

    for i in range(8):
        for condition, copies in sends(i):
            run(condition, copies, "wait_send")
    for copy in rows_sent + weights_sent + parts_sent + updates_sent:
        copy.wait_send()


def per_device(
    query_single, query_frames, query_chain, key_single, key_frames, key_chain, key_mask, pair,
    w_q, w_k, w_v, w_qp, w_kp, w_vp, w_bias, head_weight, chain_bias, w_out, ln_gain, w_frame,
):
    chain_q = query_chain.astype(F32)[None]
    meta_q = jnp.concatenate([query_frames, chain_q, jnp.zeros((3, 16), F32)], axis=0)
    codes = jnp.stack([key_chain, key_mask]).astype(F32)
    meta_k = jnp.concatenate([key_frames, codes, jnp.zeros((2, 192), F32)], axis=0)
    meta_k = jnp.pad(meta_k, ((0, 0), (0, 64)))
    pair = pair.reshape(16, CHUNKS, KEYS, 128)
    vm = pltpu.VMEM
    anywhere = pl.BlockSpec(memory_space=pl.ANY)
    scalars = pl.BlockSpec(memory_space=pltpu.SMEM)
    inside = pl.BlockSpec(memory_space=pltpu.VMEM)
    return pl.pallas_call(
        kernel,
        out_shape=(jax.ShapeDtypeStruct((16, 384), BF16), jax.ShapeDtypeStruct((12, 16), F32)),
        in_specs=[anywhere] * 15 + [scalars] * 2,
        out_specs=(inside, inside),
        scratch_shapes=[
            vm((16, 384), BF16), vm((16, 16), F32), vm((384, 48), BF16), vm((384, 48), BF16),
            vm((384, 48), BF16), vm((384, 36), BF16), vm((384, 36), BF16), vm((384, 72), BF16),
            vm((128, 12), BF16), vm((528, 384), BF16), vm((1, 384), F32), vm((384, 6), BF16),
            vm((16, CHUNKS, KEYS, 128), BF16), vm((CHUNKS, 2, 192, 384), BF16), vm((CHUNKS, 2, 16, 256), F32),
            vm((CHUNKS, GROUPS, GROUP, KEYS), F32), vm((4, 48, 512), BF16), vm((4, 176, 384), BF16),
            vm((ROWS, 384), BF16), vm((ROWS, 512), BF16), vm((ROWS, 384), BF16), vm((ROWS, 384), BF16),
            vm((288, 384), BF16), vm((16, 1), F32), vm((32, 256), BF16),
            vm((GROUPS, GROUP, 128), F32), vm((ROWS, 384), F32), vm((ROWS, 288), F32),
            vm((ROWS, 1), F32), vm((ROWS, 1), F32),
            vm((4, 48, 256), BF16), vm((4, 48, 256), BF16), vm((4, 16, 384), F32),
            pltpu.SemaphoreType.DMA((14,)), pltpu.SemaphoreType.DMA((GROUPS,)),
            pltpu.SemaphoreType.DMA((64,)), pltpu.SemaphoreType.DMA((64,)),
        ],
        compiler_params=pltpu.CompilerParams(
            collective_id=0, has_side_effects=True, vmem_limit_bytes=56 * 1024 * 1024
        ),
    )(
        query_single, meta_q, key_single, meta_k, pair, w_q, w_k, w_v, w_qp, w_kp, w_vp, w_bias, w_out,
        ln_gain[None], w_frame, head_weight, chain_bias,
    )


def solution(mesh):
    rows = ("sample", "blk")
    heads = P(None, "head")
    in_specs = (
        P(rows, None), P(None, rows), P(rows), P(rows, None), P(None, rows), P(rows), P(rows),
        P(rows, "head", None), heads, heads, heads, heads, heads, heads, P(), P("head"), P("head"),
        P(), P(), P(),
    )
    out_specs = (P(rows, None), P(None, rows))
    return jax.shard_map(
        per_device, mesh=mesh, in_specs=in_specs, out_specs=out_specs, check_vma=False
    )
```

```python
import math

import jax
import jax.numpy as jnp
from jax import lax
from jax.experimental import pallas as pl
from jax.experimental.pallas import tpu as pltpu
from jax.sharding import PartitionSpec as P

F32 = jnp.float32
BF16 = jnp.bfloat16
HIGH = lax.Precision.HIGHEST
MESH = pl.DeviceIdType.MESH

HEADS = 12
QPTS = 4
ROWS = 192
GROUPS = 8
GROUP = 24
EVENTS = {
    "z0": (0, 0, 0), "z1": (0, 1, 0), "l0": (1, 0, 0), "r0": (2, 0, 0), "z2": (0, 0, 1), "l1": (1, 1, 0),
    "r1": (2, 1, 0), "z3": (0, 1, 1), "l2": (1, 0, 1), "r2": (2, 0, 1), "l3": (1, 1, 1), "r3": (2, 1, 1),
    "o0": (3, 0, 1), "o1": (3, 1, 1),
}
SLOTS = {
    "z0": (-1, 4, 8), "z1": (4, 6, 8), "l0": (4, 8, 8), "r0": (4, 8, 8), "z2": (-1, 8, 8), "l1": (7, 8, 8),
    "r1": (7, 8, 8), "z3": (6, 8, 8), "l2": (5, 9, 9), "r2": (5, 9, 9), "l3": (8, 9, 9), "r3": (8, 9, 9),
    "o0": (10, 10, 10), "o1": (11, 11, 11),
}
CHUNKS = 8
KEYS = 384
WEIGHT_L = math.sqrt(1.0 / 3.0)
WEIGHT_C = math.sqrt(2.0 / (9.0 * QPTS))

Z_IN, LEFT_IN, RIGHT_IN, HALF_LEFT_IN, HALF_RIGHT_IN, CORE_IN = 0, 4, 8, 12, 14, 16
ROWS_IN, WEIGHTS_IN, PART_IN, META = 24, 27, 30, 33
Z_OUT, Z_BACK, Z_LAST, RIGHT_OUT, LEFT_OUT, HALF_RIGHT_OUT, HALF_LEFT_OUT, CORE_OUT = 0, 4, 8, 12, 16, 20, 22, 24
ROWS_OUT, WEIGHTS_OUT, PART_OUT, META_OUT = 32, 35, 38, 41


def iota(shape, dim):
    return lax.broadcasted_iota(jnp.int32, shape, dim)


def by3(v):
    return (v * 171) >> 9


def by12(v):
    return (v * 171) >> 11


def by24(v):
    return (v * 2731) >> 16


def by48(v):
    return (v * 1366) >> 16


def by80(v):
    return (v * 820) >> 16


def by96(v):
    return (v * 683) >> 16


def ones_where(cond, dtype=BF16):
    return jnp.where(cond, 1.0, 0.0).astype(dtype)


def mm(lhs, rhs, precision=None):
    return lax.dot_general(
        lhs, rhs, (((1,), (0,)), ((), ())), precision=precision, preferred_element_type=F32
    )


def nt(lhs, rhs, precision=None):
    return lax.dot_general(
        lhs, rhs, (((1,), (1,)), ((), ())), precision=precision, preferred_element_type=F32
    )


def short(v):
    return v.astype(BF16).astype(F32)


def split2(v):
    first = short(v)
    return first, short(v - first)


def split3(v):
    first = short(v)
    second = short(v - first)
    return first, second, short(v - first - second)


def head16(head):
    owner = by3(head)
    return owner * 4 + head - owner * 3


def quat_rotation(w, x, y, z):
    return [
        1.0 - 2.0 * (y * y + z * z),
        2.0 * (x * y - w * z),
        2.0 * (x * z + w * y),
        2.0 * (x * y + w * z),
        1.0 - 2.0 * (x * x + z * z),
        2.0 * (y * z - w * x),
        2.0 * (x * z - w * y),
        2.0 * (y * z + w * x),
        1.0 - 2.0 * (x * x + y * y),
    ]


def own_rows(single, frames, chain, w_q, w_k, w_qp, head_weight, chain_bias):
    rows = 48
    row = iota((rows, 1), 0)
    query = by3(row)
    local_head = row - query * 3
    spread = query == iota((rows, 16), 1)
    single_rows = mm(ones_where(spread), single).astype(BF16)
    q_s = nt(single_rows, w_q).astype(BF16).astype(F32)
    col = iota((rows, 48), 1)
    q_s = jnp.where((col >> 4) == local_head, q_s, 0.0).astype(BF16)
    scalar = mm(q_s, w_k) * (WEIGHT_L / 4.0)

    frames = nt(ones_where(spread, F32), frames, HIGH)
    own_chain = jnp.sum(jnp.where(spread, chain.astype(F32), 0.0), axis=1, keepdims=True)
    local = nt(single_rows, w_qp)
    col = iota((rows, 36), 1)
    local = jnp.where(by12(col) == local_head, local, 0.0)
    lane = iota((1, 128), 1)
    comp = jnp.where(lane < 12, lane, lane - 12)
    axis = comp >> 2
    point = comp & 3
    inside = lane < 24
    source = iota((36, 128), 0)
    source = source - by12(source) * 12
    entry = iota((12, 128), 0)
    placed = mm(frames, ones_where((entry == axis + 9) & inside, F32), HIGH)
    for b in range(3):
        here = mm(local, ones_where((source == point + 4 * b) & inside, F32), HIGH)
        turn = mm(frames, ones_where((entry == axis * 3 + b) & inside, F32), HIGH)
        placed = placed + turn * here
    norm = jnp.sum(jnp.where(lane < 12, placed * placed, 0.0), axis=1, keepdims=True)

    def per_head(ref):
        return jnp.where(local_head == 0, ref[0], jnp.where(local_head == 1, ref[1], ref[2]))

    weight = per_head(head_weight)
    soft = jnp.maximum(weight, 0.0) + jnp.log(1.0 + jnp.exp(-jnp.abs(weight)))
    coeff = soft * (WEIGHT_L * WEIGHT_C / 2.0)
    point_hi, point_lo = split2(2.0 * coeff * placed)
    chain_hi, chain_lo = split2(per_head(chain_bias) * WEIGHT_L)
    lane_f = lane.astype(F32)
    compact = jnp.where(lane < 12, point_hi, jnp.where(inside, point_lo, 0.0))
    compact = jnp.where((lane >= 24) & (lane < 48) & (own_chain == lane_f - 24.0), chain_hi, compact)
    compact = jnp.where((lane >= 48) & (lane < 72) & (own_chain == lane_f - 48.0), chain_lo, compact)
    for first, values in ((72, split3(-coeff * norm)), (75, split3(coeff))):
        for step, value in enumerate(values):
            compact = jnp.where(lane == first + step, value, compact)
    return scalar.astype(BF16), compact.astype(BF16)


def own_weights(w_kp, w_v, w_vp):
    row = iota((48, 36), 0)
    col = iota((48, 36), 1)
    head = row & 3
    pick = (col == head * 12 + (row >> 4) * 4 + ((row >> 2) & 3)) & (head < 3)
    key_points = mm(ones_where(pick), w_kp).astype(BF16)
    row = iota((80, 72), 0)
    col = iota((80, 72), 1)
    b = by24(row)
    rest = row - b * 24
    pick = (col == (rest >> 3) * 24 + b * 8 + (rest & 7)) & (row < 72)
    value_points = mm(ones_where(pick), w_vp).astype(BF16)
    return key_points, w_v, value_points


def all_rows(packs):
    shape = (ROWS, ROWS)
    row, col = iota(shape, 0), iota(shape, 1)
    query = by12(row)
    owner = by48(col)
    rest = col - owner * 48
    col_query = by3(rest)
    pick = (query == col_query) & (row - query * 12 == owner * 3 + rest - col_query * 3)
    rows = mm(ones_where(pick), packs).astype(BF16)
    compact = rows[:, 384:]
    lane = iota((1, 512), 1)
    again = jnp.where(lane < 192, lane, lane - 192)
    source = ((again >> 6) * 4 + ((again >> 4) & 3)) + jnp.where(lane < 192, 0, 12)
    source = jnp.where(lane >= 384, -1, source)
    source = jnp.where((lane >= 384) & (lane < 408), lane - 360, source)
    source = jnp.where((lane >= 416) & (lane < 440), lane - 368, source)
    source = jnp.where((lane >= 496) & (lane < 499), lane - 424, source)
    other = mm(compact, ones_where(iota((128, 512), 0) == source))
    row = iota((ROWS, 1), 0)
    place = head16(row - by12(row) * 12)
    mine = (lane & 15) == place
    other = jnp.where(mine | (lane >= 384), other, 0.0)
    other = jnp.where(mine & (lane >= 448) & (lane < 496), 1.0, other)
    spot, col = iota((16, ROWS), 0), iota((16, ROWS), 1)
    pick = (head16(col) == spot) & (col < 12)
    factors = mm(ones_where(pick), compact)
    factor = factors[:, 75:76] + factors[:, 76:77] + factors[:, 77:78]
    return rows[:, :384], other.astype(BF16), factor


def kernel(
    single_q, frames_q, chain_q, single_k, frames_k, chain_k, mask_k, pair, w_q, w_k, w_v, w_qp, w_kp, w_vp, w_bias,
    w_out, head_weight, chain_bias,
    mixed_out,
    v_single, v_frames, v_chain, v_kframes, v_kchain, v_kmask, v_wq, v_wk, v_wv, v_wqp, v_wkp, v_wvp, v_wbias, v_wout,
    pairs, keys, metas, bias, pack_rows, pack_weights,
    rows_single, rows_other, w_points, w_values, w_vpoints, factors, bias_rows,
    acc_pair, acc_single, acc_points, top, total, part_in,
    local_sem, pair_sem, send_sem, recv_sem,
):
    y = lax.axis_index("head")
    blk = lax.axis_index("blk")
    z = lax.div(blk, 8)
    core = lax.rem(blk, 2)
    x = lax.rem(lax.div(blk, 2), 4)
    r = lax.rem(z - 2 * y + 8, 8)
    upper = (r >= 1) & (r <= 4)
    depth = jnp.where(r <= 1, 0, jnp.where((r == 3) | (r == 6), 1, 2))
    near = jnp.where(upper, 1, 0)

    def device(zz, xx, cc):
        return (zz * 4 + xx) * 2 + cc

    partner = device(lax.rem(z + jnp.where(r == 0, 1, 7), 8), x, core)
    above, below = device(lax.rem(z + 1, 8), x, core), device(lax.rem(z + 7, 8), x, core)
    first_relay = device(lax.rem(2 * y + 3, 8), x, core)
    second_relay = device(lax.rem(2 * y + 6, 8), x, core)
    right = device(z, lax.rem(x + 1, 4), core)
    left = device(z, lax.rem(x + 3, 4), core)
    sibling = device(z, x, 1 - core)

    small = [
        (single_q, v_single), (frames_q, v_frames), (chain_q, v_chain), (w_q, v_wq), (w_k, v_wk), (w_qp, v_wqp),
        (w_kp, v_wkp), (w_v, v_wv), (w_vp, v_wvp), (w_bias, v_wbias),
    ]
    small = [pltpu.make_async_copy(src, dst, local_sem.at[i]) for i, (src, dst) in enumerate(small)]

    def item(phase, kind):
        plane = near if phase == 0 else 1 - near
        return plane * 4 + lax.rem(x + (0, 3, 1, 2)[kind], 4)

    def chunk_of(phase, kind):
        return (phase, 2 + 2 * phase, 3 + 2 * phase, 6 + phase)[kind]

    own_index = item(0, 0)
    own_copies = [
        pltpu.make_async_copy(src, dst, local_sem.at[10 + i])
        for i, (src, dst) in enumerate(
            ((single_k, keys.at[own_index, core]), (frames_k, v_kframes), (chain_k, v_kchain), (mask_k, v_kmask))
        )
    ]
    out_copy = pltpu.make_async_copy(w_out, v_wout, local_sem.at[14])
    pair_copies = [
        pltpu.make_async_copy(pair.at[pl.ds(2 * g, 2)], pairs.at[pl.ds(2 * g, 2)], pair_sem.at[g])
        for g in range(GROUPS)
    ]

    barrier = pltpu.get_barrier_semaphore()
    along_z = [(depth == 0, partner), (depth == 0, first_relay), (depth == 0, second_relay)]
    along_z += [(depth == 1, above), (depth == 1, below)]
    along_z += [(depth == 1, device(lax.rem(2 * y, 8), x, core)), (depth == 1, device(lax.rem(2 * y + 1, 8), x, core))]
    along_z += [(depth == 2, device(lax.rem(2 * y + jnp.where(upper, 3, 6), 8), x, core))]
    for condition, other in along_z:

        @pl.when(condition)
        def _(other=other):
            pl.semaphore_signal(barrier, inc=1, device_id={"blk": other}, device_id_type=MESH)

    for other in (right, left, sibling):
        pl.semaphore_signal(barrier, inc=1, device_id={"blk": other}, device_id_type=MESH)
    for step in (1, 2, 3):
        pl.semaphore_signal(
            barrier, inc=1, device_id={"head": lax.rem(y + step, 4)}, device_id_type=MESH
        )

    @pl.when(depth == 0)
    def _():
        for copy in own_copies:
            copy.start()

    for copy in small:
        copy.start()
    for copy in pair_copies:
        copy.start()
    out_copy.start()

    def remote(src, dst, sent, received, target):
        return pltpu.make_async_remote_copy(
            src_ref=src, dst_ref=dst, send_sem=send_sem.at[sent], recv_sem=recv_sem.at[received],
            device_id=target, device_id_type=MESH,
        )

    def block(index, cc, sent, received, target, half=None, meta=True):
        ref = keys.at[index, cc]
        if half is not None:
            ref = keys.at[index, cc, pl.ds(96 * half, 96)]
        copies = [remote(ref, ref, sent, received, {"blk": target})]
        if meta:
            ref = metas.at[index, cc]
            copies.append(remote(ref, ref, sent + META_OUT, received + META, {"blk": target}))
        return copies

    def sends(name):
        kind, phase, half = EVENTS[name]
        index = item(phase, kind)
        result = []
        step = 2 * phase + half
        meta = half == 0

        def add(condition, sent, received, target):
            result.append((condition, block(index, core, sent, received, target, half, meta)))

        if kind == 0:
            if phase == 0:
                far = Z_IN + 2 + half
                add(depth == 0, Z_OUT + half, far, partner)
                add(r == 1, Z_BACK + half, Z_IN + half, first_relay)
                add(r == 1, Z_LAST + half, far, second_relay)
                add(r == 0, Z_BACK + half, Z_IN + half, second_relay)
                add(r == 0, Z_LAST + half, far, first_relay)
            add(depth == 1, Z_OUT + step, Z_IN + step, above)
            add(depth == 1, Z_BACK + step, Z_IN + step, below)
            add(None, RIGHT_OUT + step, LEFT_IN + step, right)
            add(None, LEFT_OUT + step, RIGHT_IN + step, left)
        if kind == 1 and half == 0:
            add(None, HALF_RIGHT_OUT + phase, HALF_LEFT_IN + phase, right)
        if kind == 2 and half == 1:
            add(None, HALF_LEFT_OUT + phase, HALF_RIGHT_IN + phase, left)
        if half == 1:
            i = chunk_of(phase, kind)
            result.append((None, block(index, core, CORE_OUT + i, CORE_IN + i, sibling)))
        return result

    def run(condition, copies, verb):
        def act():
            for copy in copies:
                getattr(copy, verb)()

        if condition is None:
            act()
        else:
            pl.when(condition)(act)

    def event(name):
        kind, phase, half = EVENTS[name]
        index = item(phase, kind)
        step = 2 * phase + half
        if kind == 3:
            arriving = block(index, core, 0, HALF_LEFT_IN + phase, sibling, 0)
            arriving += block(index, core, 0, HALF_RIGHT_IN + phase, sibling, 1, False)
        else:
            place = (Z_IN, LEFT_IN, RIGHT_IN)[kind] + step
            arriving = block(index, core, 0, place, sibling, half, half == 0)
        run(depth > 0 if kind == 0 and phase == 0 else None, arriving, "wait_recv")
        for condition, copies in sends(name):
            run(condition, copies, "start")

    slots = {
        name: jnp.where(depth == 0, when[0], jnp.where(depth == 1, when[1], when[2])) for name, when in SLOTS.items()
    }

    def events_at(step, names):
        for name in names:
            pl.when(slots[name] == step)(lambda name=name: event(name))

    @pl.when(depth == 0)
    def _():
        for copy in own_copies:
            copy.wait()
        metas[own_index, core] = jnp.zeros((16, 256), F32)
        metas[own_index, core, :12, :192] = v_kframes[...]
        metas[own_index, core, 12:13, :192] = v_kchain[...].astype(F32)
        metas[own_index, core, 13:14, :192] = v_kmask[...].astype(F32)

    pl.semaphore_wait(barrier, jnp.where(depth == 0, 9, jnp.where(depth == 1, 10, 7)))
    events_at(-1, ["z0", "z2"])

    for copy in small:
        copy.wait()
    scalar, compact = own_rows(
        v_single[...], v_frames[...], v_chain[...], v_wq[...], v_wk[...], v_wqp[...], head_weight, chain_bias
    )
    pack_rows[y, :, :384] = scalar
    pack_rows[y, :, 384:] = compact
    key_points, values, value_points = own_weights(v_wkp[...], v_wv[...], v_wvp[...])
    pack_weights[y, :48] = key_points
    pack_weights[y, 48:96] = values
    pack_weights[y, 96:] = value_points

    def exchange(src, dst, sent, received):
        out, arriving = [], []
        for step in (1, 2, 3):
            peer = lax.rem(y + step, 4)
            origin = lax.rem(y + 4 - step, 4)
            out.append(remote(src(peer), dst.at[y], sent + step - 1, received + step - 1, {"head": peer}))
            arriving.append(
                remote(dst.at[origin], dst.at[origin], sent + step - 1, received + step - 1, {"head": peer})
            )
        return out, arriving

    rows_sent, rows_arriving = exchange(lambda peer: pack_rows.at[y], pack_rows, ROWS_OUT, ROWS_IN)
    weights_sent, weights_arriving = exchange(
        lambda peer: pack_weights.at[y], pack_weights, WEIGHTS_OUT, WEIGHTS_IN
    )
    for copy in rows_sent + weights_sent:
        copy.start()

    col = iota((32, 12), 1)
    pick_row = iota((32, 12), 0)
    first = mm(ones_where(pick_row == col), v_wbias[...])
    second = mm(ones_where(pick_row == col + 12), v_wbias[...])
    bias_rows[:, :128] = first.astype(BF16)
    bias_rows[:, 128:] = second.astype(BF16)

    def bias_step(t, _):
        pltpu.make_async_copy(pair.at[pl.ds(2 * t, 2)], pairs.at[pl.ds(2 * t, 2)], pair_sem.at[t]).wait()
        for c in range(0, CHUNKS, 2):
            block_a = pairs[2 * t, c : c + 2].reshape(2 * KEYS, 128)
            block_b = pairs[2 * t + 1, c : c + 2].reshape(2 * KEYS, 128)
            out = nt(bias_rows[...], jnp.concatenate([block_a, block_b], axis=1))[:GROUP]
            out = short(out) * WEIGHT_L
            bias[c, t] = out[:, :KEYS]
            bias[c + 1, t] = out[:, KEYS:]
        events_at(t, [name for name, when in SLOTS.items() if any(0 <= k < 8 for k in when)])
        return 0

    lax.fori_loop(0, GROUPS, bias_step, 0)
    events_at(8, [name for name, when in SLOTS.items() if 8 in when])

    for copy in rows_arriving + weights_arriving:
        copy.wait_recv()
    for_single, for_other, factor = all_rows(pack_rows[...].reshape(ROWS, 512))
    rows_single[...] = for_single
    rows_other[...] = for_other
    factors[...] = -factor
    packs = pack_weights[...]
    row, col = iota((ROWS, ROWS), 0), iota((ROWS, ROWS), 1)
    place = row & 15
    pick = col == (place >> 2) * 48 + (row >> 6) * 16 + ((row >> 4) & 3) * 4 + (place & 3)
    w_points[...] = mm(ones_where(pick), packs[:, :48].reshape(ROWS, 384)).astype(BF16)
    w_values[...] = packs[:, 48:96].reshape(ROWS, 384)
    row, col = iota((288, 320), 0), iota((288, 320), 1)
    b = by96(row)
    rest = row - b * 96
    owner = by24(rest)
    pick = col == owner * 80 + b * 24 + rest - owner * 24
    w_vpoints[...] = mm(ones_where(pick), packs[:, 96:].reshape(320, 384)).astype(BF16)

    acc_pair[...] = jnp.zeros_like(acc_pair)
    acc_single[...] = jnp.zeros_like(acc_single)
    acc_points[...] = jnp.zeros_like(acc_points)
    top[...] = jnp.full_like(top, -1e30)
    total[...] = jnp.zeros_like(total)

    indices = [item(*pair) for pair in ((0, 0), (1, 0), (0, 1), (0, 2), (1, 1), (1, 2), (0, 3), (1, 3))]

    def index_of(i):
        value = indices[7]
        for k in range(7):
            value = jnp.where(i == k, indices[k], value)
        return value

    def key_meta(index):
        half = iota((16, 128), 1) < 64
        first, second = metas[index, 0], metas[index, 1]
        start = pltpu.roll(second[:, :128], 64, 1)
        end = pltpu.roll(second[:, 128:], 64, 1)
        return [first[:, :128], jnp.where(half, first[:, 128:], start), jnp.where(half, start, end)]

    def key_step(s, _):
        events_at(jnp.where(s == 0, -2, s + 8), [name for name, when in SLOTS.items() if max(when) > 8])
        pair_of = []
        for k in range(2):
            i = 2 * s + k
            index = index_of(i)
            pair_of.append(index)
            here = keys.at[index, 1 - core]
            remote(here, here, 0, CORE_IN + i, {"blk": sibling}).wait_recv()
            here = metas.at[index, 1 - core]
            remote(here, here, 0, META + CORE_IN + i, {"blk": sibling}).wait_recv()

        single = jnp.concatenate([keys[index].reshape(KEYS, 384) for index in pair_of], axis=0)
        meta = jnp.concatenate(key_meta(pair_of[0]) + key_meta(pair_of[1]), axis=1)

        def placed(local, rows):
            result = []
            for a in range(3):
                moved = meta[9 + a : 10 + a] + meta[3 * a : 3 * a + 1] * local[:rows]
                moved = moved + meta[3 * a + 1 : 3 * a + 2] * local[rows : 2 * rows]
                moved = moved + meta[3 * a + 2 : 3 * a + 3] * local[2 * rows :]
                result.append(moved.astype(BF16))
            return result

        points = placed(nt(w_points[...], single), 64)
        square = 0.0
        for part in points:
            wide = part.astype(F32)
            square = square + wide * wide
        norm = square[:16] + square[16:32] + square[32:48] + square[48:]
        norms = [v.astype(BF16) for v in split3(norm * factors[...])]
        width = 2 * KEYS
        chains = ones_where(meta[12:13] == iota((32, width), 0).astype(F32))
        others = jnp.concatenate(
            points + points + [chains, chains] + norms + [jnp.full((16, width), 1.0, BF16)], axis=0
        )
        logit = nt(rows_single[...], single) + mm(rows_other[...], others)
        logit = logit + jnp.concatenate([bias[index].reshape(ROWS, KEYS) for index in pair_of], axis=1)
        logit = jnp.where(meta[13:14] > 0.5, logit, -1000000000.0)
        old = top[...]
        new = jnp.maximum(old, jnp.max(logit, axis=1, keepdims=True))
        scale = jnp.exp(old - new)
        weight = jnp.exp(logit - new)
        top[...] = new
        total[...] = total[...] * scale + jnp.sum(weight, axis=1, keepdims=True)
        weight_b = weight.astype(BF16)
        acc_single[...] = acc_single[...] * scale + mm(weight_b, single)
        vpoints = jnp.concatenate(placed(nt(w_vpoints[...], single), 96), axis=0)
        acc_points[...] = acc_points[...] * scale + nt(weight_b, vpoints)
        upper_rows = iota((GROUP, 128), 0) < 12
        for g in range(GROUPS):
            lo = g * GROUP
            there = jnp.concatenate(
                [
                    jnp.concatenate([pairs[2 * g, index] for index in pair_of], axis=0),
                    jnp.concatenate([pairs[2 * g + 1, index] for index in pair_of], axis=0),
                ],
                axis=1,
            )
            out = mm(weight[lo : lo + GROUP].astype(BF16), there)
            out = jnp.where(upper_rows, out[:, :128], out[:, 128:])
            acc_pair[g] = acc_pair[g] * scale[lo : lo + GROUP] + out
        return 0

    lax.fori_loop(0, 4, key_step, 0)

    inverse = 1.0 / total[...]
    row = iota((ROWS, 1), 0)
    query = by12(row)
    head = row - query * 12
    part_in[y, :ROWS] = (acc_pair[...].reshape(ROWS, 128) * inverse).astype(BF16)
    hi, lo = split2(acc_single[...] * inverse)
    scalar = nt(hi.astype(BF16), w_values[...]) + nt(lo.astype(BF16), w_values[...])
    scalar = jnp.where((iota((ROWS, ROWS), 1) >> 4) == head, scalar, 0.0).astype(BF16)
    lane = iota((1, 128), 1)
    again = lane & 63
    source = iota((ROWS, 128), 0)
    other = mm(scalar, ones_where(((source & 15) == again) & (again < 16)))
    frames = nt(ones_where(query == iota((ROWS, 16), 1), F32), v_frames[...], HIGH)
    col = iota((1, 288), 1)
    axis = by96(col)
    center = jnp.where(axis == 0, frames[:, 9:10], jnp.where(axis == 1, frames[:, 10:11], frames[:, 11:12]))
    shifted = jnp.where(((col - axis * 96) >> 3) == head, acc_points[...] * inverse - center, 0.0).astype(BF16)
    source = iota((288, 128), 0)
    other = other + mm(shifted, ones_where(again == by96(source) * 8 + (source & 7) + 16))
    for start, value in ((40, top[...]), (43, total[...])):
        for step, piece in enumerate(split3(value)):
            other = jnp.where(again == start + step, piece, other)
    half = ROWS // 2
    part_in[y, ROWS:] = jnp.where(lane < 64, other[:half], other[half:]).astype(BF16)

    parts_sent, parts_arriving = exchange(lambda peer: part_in.at[y], part_in, PART_OUT, PART_IN)
    for copy in parts_sent:
        copy.start()
    for copy in parts_arriving:
        copy.wait_recv()

    pair_parts = [part_in[k, :ROWS].astype(F32) for k in range(4)]
    others = []
    for k in range(4):
        both = part_in[k, ROWS:].astype(F32)
        others.append(jnp.concatenate([both, pltpu.roll(both, 64, 1)], axis=0))
    tops = [p[:, 40:41] + p[:, 41:42] + p[:, 42:43] for p in others]
    best = jnp.maximum(jnp.maximum(tops[0], tops[1]), jnp.maximum(tops[2], tops[3]))
    shares = [
        (p[:, 43:44] + p[:, 44:45] + p[:, 45:46]) * jnp.exp(t - best) for p, t in zip(others, tops)
    ]
    inverse = 1.0 / (shares[0] + shares[1] + shares[2] + shares[3])
    shares = [share * inverse for share in shares]
    o_pair = sum(p * s for p, s in zip(pair_parts, shares)).astype(BF16)
    other = sum(p * s for p, s in zip(others, shares))
    inside = (lane >= 16) & (lane < 40)
    axis = (lane - 16) >> 3
    point = lane & 7
    source = iota((128, 128), 0)
    entry = iota((12, 128), 0)
    located = 0.0
    for b in range(3):
        pick = (source == point + 16 + 8 * b) & inside
        turn = mm(frames, ones_where((entry == 3 * b + axis) & inside, F32), HIGH)
        located = located + turn * mm(other, ones_where(pick, F32), HIGH)
    last = (lane >= 40) & (lane < 48)
    pick = (source >= 16) & (source < 40) & ((source & 7) == point) & last
    length = jnp.sqrt(mm(located * located, ones_where(pick, F32), HIGH) + 1e-08)
    feats = jnp.where(lane < 16, other, jnp.where(inside, located, jnp.where(last, length, 0.0)))
    feats = jnp.concatenate([o_pair, feats.astype(BF16)], axis=1)
    row, col = iota((ROWS, ROWS), 0), iota((ROWS, ROWS), 1)
    query = by12(col)
    pick = ones_where(((row & 15) == query) & ((row >> 4) == col - query * 12))
    feats = mm(pick, feats).astype(BF16)
    out_copy.wait()
    update = v_single[...].astype(F32)
    for k in range(HEADS):
        here = feats[16 * k : 16 * k + 16]
        w = 176 * k
        update = update + mm(here[:, :128], v_wout[w + 16 : w + 144])
        rest = jnp.concatenate([v_wout[w : w + 16], v_wout[w + 144 : w + 176]], axis=0)
        update = update + mm(here[:, 128:176], rest)
    mixed_out[...] = update

    for name in EVENTS:
        for condition, copies in sends(name):
            run(condition, copies, "wait_send")
    for copy in rows_sent + weights_sent + parts_sent:
        copy.wait_send()


def finish(mixed_ref, gain, w_frame, frames, single_out, frames_out):
    mixed = mixed_ref[...]
    mean = jnp.mean(mixed, axis=1, keepdims=True)
    centered = mixed - mean
    var = jnp.mean(centered * centered, axis=1, keepdims=True)
    out = (centered / jnp.sqrt(var + 1e-05) * gain[...][None]).astype(BF16)
    single_out[...] = out
    shift = nt(w_frame[...], out)
    u = [shift[k : k + 1] for k in range(6)]
    length = jnp.sqrt(1.0 + u[0] * u[0] + u[1] * u[1] + u[2] * u[2])
    turn = quat_rotation(1.0 / length, u[0] / length, u[1] / length, u[2] / length)
    rot = [frames[k : k + 1] for k in range(12)]
    for a in range(3):
        for c in range(3):
            k = 3 * a + c
            frames_out[k : k + 1] = (
                rot[3 * a] * turn[c] + rot[3 * a + 1] * turn[3 + c] + rot[3 * a + 2] * turn[6 + c]
            )
        moved = rot[3 * a] * u[3] + rot[3 * a + 1] * u[4] + rot[3 * a + 2] * u[5]
        frames_out[9 + a : 10 + a] = moved + rot[9 + a]


def per_device(
    query_single, query_frames, query_chain, key_single, key_frames, key_chain, key_mask, pair,
    w_q, w_k, w_v, w_qp, w_kp, w_vp, w_bias, head_weight, chain_bias, w_out, ln_gain, w_frame,
):
    pair = pair.reshape(16, CHUNKS, KEYS, 128)
    vm = pltpu.VMEM
    anywhere = pl.BlockSpec(memory_space=pl.ANY)
    scalars = pl.BlockSpec(memory_space=pltpu.SMEM)
    inside = pl.BlockSpec(memory_space=pltpu.VMEM)
    mixed = pl.pallas_call(
        kernel,
        out_shape=jax.ShapeDtypeStruct((16, 384), F32),
        in_specs=[anywhere] * 16 + [scalars] * 2,
        out_specs=inside,
        scratch_shapes=[
            vm((16, 384), BF16), vm((12, 16), F32), vm((1, 16), jnp.int32), vm((12, 192), F32),
            vm((1, 192), jnp.int32), vm((1, 192), jnp.int32), vm((48, 384), BF16), vm((48, 384), BF16),
            vm((48, 384), BF16), vm((36, 384), BF16), vm((36, 384), BF16), vm((72, 384), BF16),
            vm((12, 128), BF16), vm((2112, 384), BF16),
            vm((16, CHUNKS, KEYS, 128), BF16), vm((CHUNKS, 2, 192, 384), BF16), vm((CHUNKS, 2, 16, 256), F32),
            vm((CHUNKS, GROUPS, GROUP, KEYS), F32), vm((4, 48, 512), BF16), vm((4, 176, 384), BF16),
            vm((ROWS, 384), BF16), vm((ROWS, 512), BF16), vm((ROWS, 384), BF16), vm((ROWS, 384), BF16),
            vm((288, 384), BF16), vm((16, 1), F32), vm((32, 256), BF16),
            vm((GROUPS, GROUP, 128), F32), vm((ROWS, 384), F32), vm((ROWS, 288), F32),
            vm((ROWS, 1), F32), vm((ROWS, 1), F32), vm((4, 288, 128), BF16),
            pltpu.SemaphoreType.DMA((15,)), pltpu.SemaphoreType.DMA((GROUPS,)),
            pltpu.SemaphoreType.DMA((80,)), pltpu.SemaphoreType.DMA((64,)),
        ],
        compiler_params=pltpu.CompilerParams(
            collective_id=0, has_side_effects=True, vmem_limit_bytes=56 * 1024 * 1024
        ),
    )(
        query_single, query_frames, query_chain[None], key_single, key_frames, key_chain[None], key_mask[None], pair,
        w_q.T, w_k.T, w_v.T, w_qp.T, w_kp.T, w_vp.T, w_bias.T, w_out, head_weight, chain_bias,
    )
    return pl.pallas_call(
        finish,
        out_shape=(jax.ShapeDtypeStruct((16, 384), BF16), jax.ShapeDtypeStruct((12, 16), F32)),
        in_specs=[inside] * 4,
        out_specs=(inside, inside),
    )(mixed, ln_gain, w_frame.T, query_frames)


def solution(mesh):
    rows = ("sample", "blk")
    heads = P(None, "head")
    in_specs = (
        P(rows, None), P(None, rows), P(rows), P(rows, None), P(None, rows), P(rows), P(rows),
        P(rows, "head", None), heads, heads, heads, heads, heads, heads, P(), P("head"), P("head"),
        P(), P(), P(),
    )
    out_specs = (P(rows, None), P(None, rows))
    return jax.shard_map(
        per_device, mesh=mesh, in_specs=in_specs, out_specs=out_specs, check_vma=False
    )
```

```python
import math

import jax
import jax.numpy as jnp
from jax import lax
from jax.experimental import pallas as pl
from jax.experimental.pallas import tpu as pltpu
from jax.sharding import PartitionSpec as P

F32 = jnp.float32
BF16 = jnp.bfloat16
HIGH = lax.Precision.HIGHEST
MESH = pl.DeviceIdType.MESH

HEADS = 12
QPTS = 4
ROWS = 192
GROUPS = 8
GROUP = 24
EVENTS = {
    "z0": (0, 0, 0), "z1": (0, 1, 0), "l0": (1, 0, 0), "r0": (2, 0, 0), "z2": (0, 0, 1), "l1": (1, 1, 0),
    "r1": (2, 1, 0), "z3": (0, 1, 1), "l2": (1, 0, 1), "r2": (2, 0, 1), "l3": (1, 1, 1), "r3": (2, 1, 1),
    "o0": (3, 0, 1), "o1": (3, 1, 1),
}
SLOTS = {
    "z0": (-1, 3, 9), "z1": (3, 5, 9), "l0": (4, 9, 9), "r0": (4, 9, 9), "z2": (1, 8, 9), "l1": (9, 9, 9),
    "r1": (9, 9, 9), "z3": (8, 8, 9), "l2": (11, 11, 11), "r2": (11, 11, 11), "l3": (11, 11, 11),
    "r3": (11, 11, 11), "o0": (12, 12, 12), "o1": (13, 13, 13),
}
CHUNKS = 8
KEYS = 384
WEIGHT_L = math.sqrt(1.0 / 3.0)
WEIGHT_C = math.sqrt(2.0 / (9.0 * QPTS))

Z_IN, LEFT_IN, RIGHT_IN, HALF_LEFT_IN, HALF_RIGHT_IN, CORE_IN = 0, 4, 8, 12, 14, 16
ROWS_IN, WEIGHTS_IN, PART_IN, META = 24, 27, 30, 33
Z_OUT, Z_BACK, Z_LAST, RIGHT_OUT, LEFT_OUT, HALF_RIGHT_OUT, HALF_LEFT_OUT, CORE_OUT = 0, 4, 8, 12, 16, 20, 22, 24
ROWS_OUT, WEIGHTS_OUT, PART_OUT, META_OUT = 32, 35, 38, 41


def iota(shape, dim):
    return lax.broadcasted_iota(jnp.int32, shape, dim)


def by3(v):
    return (v * 171) >> 9


def by12(v):
    return (v * 171) >> 11


def by24(v):
    return (v * 2731) >> 16


def by48(v):
    return (v * 1366) >> 16


def by80(v):
    return (v * 820) >> 16


def by96(v):
    return (v * 683) >> 16


def ones_where(cond, dtype=BF16):
    return jnp.where(cond, 1.0, 0.0).astype(dtype)


def mm(lhs, rhs, precision=None):
    return lax.dot_general(
        lhs, rhs, (((1,), (0,)), ((), ())), precision=precision, preferred_element_type=F32
    )


def nt(lhs, rhs, precision=None):
    return lax.dot_general(
        lhs, rhs, (((1,), (1,)), ((), ())), precision=precision, preferred_element_type=F32
    )


def short(v):
    return v.astype(BF16).astype(F32)


def split2(v):
    first = short(v)
    return first, short(v - first)


def split3(v):
    first = short(v)
    second = short(v - first)
    return first, second, short(v - first - second)


def head16(head):
    owner = by3(head)
    return owner * 4 + head - owner * 3


def quat_rotation(w, x, y, z):
    return [
        1.0 - 2.0 * (y * y + z * z),
        2.0 * (x * y - w * z),
        2.0 * (x * z + w * y),
        2.0 * (x * y + w * z),
        1.0 - 2.0 * (x * x + z * z),
        2.0 * (y * z - w * x),
        2.0 * (x * z - w * y),
        2.0 * (y * z + w * x),
        1.0 - 2.0 * (x * x + y * y),
    ]


def own_rows(single, frames, chain, w_q, w_k, w_qp, head_weight, chain_bias):
    rows = 48
    row = iota((rows, 1), 0)
    query = by3(row)
    local_head = row - query * 3
    spread = query == iota((rows, 16), 1)
    single_rows = mm(ones_where(spread), single).astype(BF16)
    q_s = nt(single_rows, w_q).astype(BF16).astype(F32)
    col = iota((rows, 48), 1)
    q_s = jnp.where((col >> 4) == local_head, q_s, 0.0).astype(BF16)
    scalar = mm(q_s, w_k) * (WEIGHT_L / 4.0)

    frames = nt(ones_where(spread, F32), frames, HIGH)
    own_chain = jnp.sum(jnp.where(spread, chain.astype(F32), 0.0), axis=1, keepdims=True)
    local = nt(single_rows, w_qp)
    col = iota((rows, 36), 1)
    local = jnp.where(by12(col) == local_head, local, 0.0)
    lane = iota((1, 128), 1)
    comp = jnp.where(lane < 12, lane, lane - 12)
    axis = comp >> 2
    point = comp & 3
    inside = lane < 24
    source = iota((36, 128), 0)
    source = source - by12(source) * 12
    entry = iota((12, 128), 0)
    placed = mm(frames, ones_where((entry == axis + 9) & inside, F32), HIGH)
    for b in range(3):
        here = mm(local, ones_where((source == point + 4 * b) & inside, F32), HIGH)
        turn = mm(frames, ones_where((entry == axis * 3 + b) & inside, F32), HIGH)
        placed = placed + turn * here
    norm = jnp.sum(jnp.where(lane < 12, placed * placed, 0.0), axis=1, keepdims=True)

    def per_head(ref):
        return jnp.where(local_head == 0, ref[0], jnp.where(local_head == 1, ref[1], ref[2]))

    weight = per_head(head_weight)
    soft = jnp.maximum(weight, 0.0) + jnp.log(1.0 + jnp.exp(-jnp.abs(weight)))
    coeff = soft * (WEIGHT_L * WEIGHT_C / 2.0)
    point_hi, point_lo = split2(2.0 * coeff * placed)
    chain_hi, chain_lo = split2(per_head(chain_bias) * WEIGHT_L)
    lane_f = lane.astype(F32)
    compact = jnp.where(lane < 12, point_hi, jnp.where(inside, point_lo, 0.0))
    compact = jnp.where((lane >= 24) & (lane < 48) & (own_chain == lane_f - 24.0), chain_hi, compact)
    compact = jnp.where((lane >= 48) & (lane < 72) & (own_chain == lane_f - 48.0), chain_lo, compact)
    for first, values in ((72, split3(-coeff * norm)), (75, split3(coeff))):
        for step, value in enumerate(values):
            compact = jnp.where(lane == first + step, value, compact)
    return scalar.astype(BF16), compact.astype(BF16)


def own_weights(w_kp, w_v, w_vp):
    row = iota((48, 36), 0)
    col = iota((48, 36), 1)
    head = row & 3
    pick = (col == head * 12 + (row >> 4) * 4 + ((row >> 2) & 3)) & (head < 3)
    key_points = mm(ones_where(pick), w_kp).astype(BF16)
    row = iota((80, 72), 0)
    col = iota((80, 72), 1)
    b = by24(row)
    rest = row - b * 24
    pick = (col == (rest >> 3) * 24 + b * 8 + (rest & 7)) & (row < 72)
    value_points = mm(ones_where(pick), w_vp).astype(BF16)
    return key_points, w_v, value_points


def all_rows(packs):
    shape = (ROWS, ROWS)
    row, col = iota(shape, 0), iota(shape, 1)
    query = by12(row)
    owner = by48(col)
    rest = col - owner * 48
    col_query = by3(rest)
    pick = (query == col_query) & (row - query * 12 == owner * 3 + rest - col_query * 3)
    rows = mm(ones_where(pick), packs).astype(BF16)
    compact = rows[:, 384:]
    lane = iota((1, 512), 1)
    again = jnp.where(lane < 192, lane, lane - 192)
    source = ((again >> 6) * 4 + ((again >> 4) & 3)) + jnp.where(lane < 192, 0, 12)
    source = jnp.where(lane >= 384, -1, source)
    source = jnp.where((lane >= 384) & (lane < 408), lane - 360, source)
    source = jnp.where((lane >= 416) & (lane < 440), lane - 368, source)
    source = jnp.where((lane >= 496) & (lane < 499), lane - 424, source)
    other = mm(compact, ones_where(iota((128, 512), 0) == source))
    row = iota((ROWS, 1), 0)
    place = head16(row - by12(row) * 12)
    mine = (lane & 15) == place
    other = jnp.where(mine | (lane >= 384), other, 0.0)
    other = jnp.where(mine & (lane >= 448) & (lane < 496), 1.0, other)
    spot, col = iota((16, ROWS), 0), iota((16, ROWS), 1)
    pick = (head16(col) == spot) & (col < 12)
    factors = mm(ones_where(pick), compact)
    factor = factors[:, 75:76] + factors[:, 76:77] + factors[:, 77:78]
    return rows[:, :384], other.astype(BF16), factor


def kernel(
    single_q, frames_q, chain_q, single_k, frames_k, chain_k, mask_k, pair, w_q, w_k, w_v, w_qp, w_kp, w_vp, w_bias,
    w_out, head_weight, chain_bias,
    mixed_out,
    v_single, v_frames, v_chain, v_kframes, v_kchain, v_kmask, v_wq, v_wk, v_wv, v_wqp, v_wkp, v_wvp, v_wbias, v_wout,
    pairs, keys, metas, bias, pack_rows, pack_weights,
    projections, rows_other, w_values, factors, bias_rows,
    acc_pair, acc_single, acc_points, top, total, part_in, centers, turns,
    local_sem, pair_sem, send_sem, recv_sem,
):
    y = lax.axis_index("head")
    blk = lax.axis_index("blk")
    z = lax.div(blk, 8)
    core = lax.rem(blk, 2)
    x = lax.rem(lax.div(blk, 2), 4)
    r = lax.rem(z - 2 * y + 8, 8)
    upper = (r >= 1) & (r <= 4)
    depth = jnp.where(r <= 1, 0, jnp.where((r == 3) | (r == 6), 1, 2))
    near = jnp.where(upper, 1, 0)

    def device(zz, xx, cc):
        return (zz * 4 + xx) * 2 + cc

    partner = device(lax.rem(z + jnp.where(r == 0, 1, 7), 8), x, core)
    above, below = device(lax.rem(z + 1, 8), x, core), device(lax.rem(z + 7, 8), x, core)
    own_relay = device(lax.rem(2 * y + jnp.where(r == 1, 3, 6), 8), x, core)
    other_relay = device(lax.rem(2 * y + jnp.where(r == 1, 6, 3), 8), x, core)
    right = device(z, lax.rem(x + 1, 4), core)
    left = device(z, lax.rem(x + 3, 4), core)
    sibling = device(z, x, 1 - core)

    small = [
        (single_q, v_single), (frames_q, v_frames), (chain_q, v_chain), (w_q, v_wq), (w_k, v_wk), (w_qp, v_wqp),
        (w_kp, v_wkp), (w_v, v_wv), (w_vp, v_wvp), (w_bias, v_wbias),
    ]
    small = [pltpu.make_async_copy(src, dst, local_sem.at[i]) for i, (src, dst) in enumerate(small)]

    def item(phase, kind):
        plane = near if phase == 0 else 1 - near
        return plane * 4 + lax.rem(x + (0, 3, 1, 2)[kind], 4)

    def chunk_of(phase, kind):
        return (phase, 2 + 2 * phase, 3 + 2 * phase, 6 + phase)[kind]

    own_index = item(0, 0)
    own_copies = [
        pltpu.make_async_copy(src, dst, local_sem.at[10 + i])
        for i, (src, dst) in enumerate(
            ((frames_k, v_kframes), (chain_k, v_kchain), (mask_k, v_kmask), (single_k, keys.at[own_index, core]))
        )
    ]
    out_copy = pltpu.make_async_copy(w_out, v_wout, local_sem.at[14])
    pair_copies = [
        pltpu.make_async_copy(pair.at[pl.ds(2 * g, 2)], pairs.at[pl.ds(2 * g, 2)], pair_sem.at[g])
        for g in range(GROUPS)
    ]

    barrier = pltpu.get_barrier_semaphore()
    along_z = [(depth == 0, partner), (depth == 0, own_relay), (depth == 0, other_relay)]
    along_z += [(depth == 1, above), (depth == 1, below)]
    along_z += [(depth == 1, device(lax.rem(2 * y, 8), x, core)), (depth == 1, device(lax.rem(2 * y + 1, 8), x, core))]
    along_z += [(depth == 2, device(lax.rem(2 * y + jnp.where(upper, 3, 6), 8), x, core))]
    for condition, other in along_z:

        @pl.when(condition)
        def _(other=other):
            pl.semaphore_signal(barrier, inc=1, device_id={"blk": other}, device_id_type=MESH)

    for other in (right, left, sibling):
        pl.semaphore_signal(barrier, inc=1, device_id={"blk": other}, device_id_type=MESH)
    for step in (1, 2, 3):
        pl.semaphore_signal(
            barrier, inc=1, device_id={"head": lax.rem(y + step, 4)}, device_id_type=MESH
        )

    @pl.when(depth == 0)
    def _():
        for copy in own_copies:
            copy.start()

    for copy in small:
        copy.start()

    def remote(src, dst, sent, received, target):
        return pltpu.make_async_remote_copy(
            src_ref=src, dst_ref=dst, send_sem=send_sem.at[sent], recv_sem=recv_sem.at[received],
            device_id=target, device_id_type=MESH,
        )

    def block(index, cc, sent, received, target, half=None, meta=True, src=None):
        ref = keys.at[index, cc]
        if half is not None:
            ref = keys.at[index, cc, pl.ds(96 * half, 96)]
        copies = [remote(ref if src is None else src, ref, sent, received, {"blk": target})]
        if meta:
            ref = metas.at[index, cc]
            copies.append(remote(ref, ref, sent + META_OUT, received + META, {"blk": target}))
        return copies

    def sends(name):
        kind, phase, half = EVENTS[name]
        index = item(phase, kind)
        result = []
        step = 2 * phase + half
        meta = half == 0

        def add(condition, sent, received, target, at_end=True, src=None):
            result.append((condition, block(index, core, sent, received, target, half, meta, src), at_end))

        if kind == 0:
            if phase == 0:
                own = single_k.at[pl.ds(96 * half, 96)]
                add(depth == 0, Z_BACK + half, Z_IN + half, own_relay, False, own)
                add(depth == 0, Z_OUT + half, Z_IN + 2 + half, partner, True, own)
                add(depth == 0, RIGHT_OUT + step, LEFT_IN + step, right, True, own)
                add(depth == 0, LEFT_OUT + step, RIGHT_IN + step, left, True, own)
            add(depth == 1, Z_OUT + step, Z_IN + step, above)
            add(depth == 1, Z_BACK + step, Z_IN + step, below)
            passed = depth > 0 if phase == 0 else None
            add(passed, RIGHT_OUT + step, LEFT_IN + step, right)
            add(passed, LEFT_OUT + step, RIGHT_IN + step, left)
        if kind == 1 and half == 0:
            add(None, HALF_RIGHT_OUT + phase, HALF_LEFT_IN + phase, right)
        if kind == 2 and half == 1:
            add(None, HALF_LEFT_OUT + phase, HALF_RIGHT_IN + phase, left)
        if half == 1:
            i = chunk_of(phase, kind)
            result.append((None, block(index, core, CORE_OUT + i, CORE_IN + i, sibling), True))
        return result

    def near_copies(half):
        own = single_k.at[pl.ds(96 * half, 96)]
        return block(own_index, core, Z_BACK + half, Z_IN + half, own_relay, half, half == 0, own)

    def far_copies(half):
        own = single_k.at[pl.ds(96 * half, 96)]
        return block(own_index, core, Z_LAST + half, Z_IN + 2 + half, other_relay, half, half == 0, own)

    def run(condition, copies, verb):
        def act():
            for copy in copies:
                getattr(copy, verb)()

        if condition is None:
            act()
        else:
            pl.when(condition)(act)

    def event(name):
        kind, phase, half = EVENTS[name]
        index = item(phase, kind)
        step = 2 * phase + half
        if kind == 3:
            arriving = block(index, core, 0, HALF_LEFT_IN + phase, sibling, 0)
            arriving += block(index, core, 0, HALF_RIGHT_IN + phase, sibling, 1, False)
        else:
            place = (Z_IN, LEFT_IN, RIGHT_IN)[kind] + step
            arriving = block(index, core, 0, place, sibling, half, half == 0)
        run(depth > 0 if kind == 0 and phase == 0 else None, arriving, "wait_recv")
        for condition, copies, _ in sends(name):
            run(condition, copies, "start")

    slots = {
        name: jnp.where(depth == 0, when[0], jnp.where(depth == 1, when[1], when[2])) for name, when in SLOTS.items()
    }

    def events_at(step, names):
        for name in names:
            pl.when(slots[name] == step)(lambda name=name: event(name))

    pl.semaphore_wait(barrier, jnp.where(depth == 0, 9, jnp.where(depth == 1, 10, 7)))
    first = [copies for condition, copies, _ in sends("z0") if condition is not None][:4]

    @pl.when(depth == 0)
    def _():
        for copies in first:
            copies[0].start()
        for copy in own_copies[:3]:
            copy.wait()
        metas[own_index, core] = jnp.zeros((16, 256), F32)
        metas[own_index, core, :12, :192] = v_kframes[...]
        metas[own_index, core, 12:13, :192] = v_kchain[...].astype(F32)
        metas[own_index, core, 13:14, :192] = v_kmask[...].astype(F32)
        for copies in first:
            copies[1].start()

    for copy in pair_copies:
        copy.start()
    out_copy.start()

    for copy in small:
        copy.wait()
    scalar, compact = own_rows(
        v_single[...], v_frames[...], v_chain[...], v_wq[...], v_wk[...], v_wqp[...], head_weight, chain_bias
    )
    pack_rows[y, :, :384] = scalar
    pack_rows[y, :, 384:] = compact
    key_points, values, value_points = own_weights(v_wkp[...], v_wv[...], v_wvp[...])
    pack_weights[y, :48] = key_points
    pack_weights[y, 48:96] = values
    pack_weights[y, 96:] = value_points

    def exchange(src, dst, sent, received):
        out, arriving = [], []
        for step in (1, 2, 3):
            peer = lax.rem(y + step, 4)
            origin = lax.rem(y + 4 - step, 4)
            out.append(remote(src(peer), dst.at[y], sent + step - 1, received + step - 1, {"head": peer}))
            arriving.append(
                remote(dst.at[origin], dst.at[origin], sent + step - 1, received + step - 1, {"head": peer})
            )
        return out, arriving

    rows_sent, rows_arriving = exchange(lambda peer: pack_rows.at[y], pack_rows, ROWS_OUT, ROWS_IN)
    weights_sent, weights_arriving = exchange(
        lambda peer: pack_weights.at[y], pack_weights, WEIGHTS_OUT, WEIGHTS_IN
    )
    for copy in rows_sent + weights_sent:
        copy.start()

    row = iota((ROWS, 16), 0)
    frames = nt(ones_where(by12(row) == iota((ROWS, 16), 1), F32), v_frames[...], HIGH)
    centers[...] = frames[:, 9:12]
    lane = iota((1, 128), 1)
    axis = (lane - 16) >> 3
    inside = (lane >= 16) & (lane < 40)
    entry = iota((12, 128), 0)
    for b in range(3):
        turns[b] = mm(frames, ones_where((entry == 3 * b + axis) & inside, F32), HIGH)

    run(depth == 0, near_copies(0), "wait_send")
    run(depth == 0, far_copies(0), "start")

    col = iota((32, 12), 1)
    pick_row = iota((32, 12), 0)
    first = mm(ones_where(pick_row == col), v_wbias[...])
    second = mm(ones_where(pick_row == col + 12), v_wbias[...])
    bias_rows[:, :128] = first.astype(BF16)
    bias_rows[:, 128:] = second.astype(BF16)

    def bias_step(t, _):
        pltpu.make_async_copy(pair.at[pl.ds(2 * t, 2)], pairs.at[pl.ds(2 * t, 2)], pair_sem.at[t]).wait()
        for c in range(0, CHUNKS, 2):
            block_a = pairs[2 * t, c : c + 2].reshape(2 * KEYS, 128)
            block_b = pairs[2 * t + 1, c : c + 2].reshape(2 * KEYS, 128)
            out = nt(bias_rows[...], jnp.concatenate([block_a, block_b], axis=1))[:GROUP]
            out = short(out) * WEIGHT_L
            bias[c, t] = out[:, :KEYS]
            bias[c + 1, t] = out[:, KEYS:]
        run((depth == 0) & (t == 1), far_copies(0), "wait_send")
        run((depth == 0) & (t == 3), near_copies(1), "wait_send")
        run((depth == 0) & (t == 3), far_copies(1), "start")
        run((depth == 0) & (t == 1), own_copies[3:], "wait")
        events_at(t, [name for name, when in SLOTS.items() if any(0 <= k < 8 for k in when)])
        return 0

    lax.fori_loop(0, GROUPS, bias_step, 0)
    events_at(8, ["z2", "z3"])
    events_at(9, [name for name, when in SLOTS.items() if 9 in when])

    for copy in rows_arriving + weights_arriving:
        copy.wait_recv()
    for_single, for_other, factor = all_rows(pack_rows[...].reshape(ROWS, 512))
    projections[:ROWS] = for_single
    rows_other[...] = for_other
    factors[...] = -factor
    packs = pack_weights[...]
    row, col = iota((ROWS, ROWS), 0), iota((ROWS, ROWS), 1)
    place = row & 15
    pick = col == (place >> 2) * 48 + (row >> 6) * 16 + ((row >> 4) & 3) * 4 + (place & 3)
    projections[ROWS : 2 * ROWS] = mm(ones_where(pick), packs[:, :48].reshape(ROWS, 384)).astype(BF16)
    w_values[...] = packs[:, 48:96].reshape(ROWS, 384)
    row, col = iota((288, 320), 0), iota((288, 320), 1)
    b = by96(row)
    rest = row - b * 96
    owner = by24(rest)
    pick = col == owner * 80 + b * 24 + rest - owner * 24
    projections[2 * ROWS :] = mm(ones_where(pick), packs[:, 96:].reshape(320, 384)).astype(BF16)

    acc_pair[...] = jnp.zeros_like(acc_pair)
    acc_single[...] = jnp.zeros_like(acc_single)
    acc_points[...] = jnp.zeros_like(acc_points)
    top[...] = jnp.full_like(top, -1e30)
    total[...] = jnp.zeros_like(total)

    indices = [item(*pair) for pair in ((0, 0), (1, 0), (0, 1), (0, 2), (1, 1), (1, 2), (0, 3), (1, 3))]

    def index_of(i):
        value = indices[7]
        for k in range(7):
            value = jnp.where(i == k, indices[k], value)
        return value

    def key_meta(index):
        half = iota((16, 128), 1) < 64
        first, second = metas[index, 0], metas[index, 1]
        start = pltpu.roll(second[:, :128], 64, 1)
        end = pltpu.roll(second[:, 128:], 64, 1)
        return [first[:, :128], jnp.where(half, first[:, 128:], start), jnp.where(half, start, end)]

    def key_step(s, _):
        events_at(s + 10, [name for name, when in SLOTS.items() if max(when) > 9])
        pair_of = []
        for k in range(2):
            i = 2 * s + k
            index = index_of(i)
            pair_of.append(index)
            here = keys.at[index, 1 - core]
            remote(here, here, 0, CORE_IN + i, {"blk": sibling}).wait_recv()
            here = metas.at[index, 1 - core]
            remote(here, here, 0, META + CORE_IN + i, {"blk": sibling}).wait_recv()

        single = jnp.concatenate([keys[index].reshape(KEYS, 384) for index in pair_of], axis=0)
        meta = jnp.concatenate(key_meta(pair_of[0]) + key_meta(pair_of[1]), axis=1)

        def placed(local, rows):
            result = []
            for a in range(3):
                moved = meta[9 + a : 10 + a] + meta[3 * a : 3 * a + 1] * local[:rows]
                moved = moved + meta[3 * a + 1 : 3 * a + 2] * local[rows : 2 * rows]
                moved = moved + meta[3 * a + 2 : 3 * a + 3] * local[2 * rows :]
                result.append(moved.astype(BF16))
            return result

        projected = nt(projections[...], single)
        points = placed(projected[ROWS : 2 * ROWS], 64)
        square = 0.0
        for part in points:
            wide = part.astype(F32)
            square = square + wide * wide
        norm = square[:16] + square[16:32] + square[32:48] + square[48:]
        norms = [v.astype(BF16) for v in split3(norm * factors[...])]
        width = 2 * KEYS
        chains = ones_where(meta[12:13] == iota((32, width), 0).astype(F32))
        others = jnp.concatenate(
            points + points + [chains, chains] + norms + [jnp.full((16, width), 1.0, BF16)], axis=0
        )
        logit = projected[:ROWS] + mm(rows_other[...], others)
        logit = logit + jnp.concatenate([bias[index].reshape(ROWS, KEYS) for index in pair_of], axis=1)
        logit = jnp.where(meta[13:14] > 0.5, logit, -1000000000.0)
        old = top[...]
        new = jnp.maximum(old, jnp.max(logit, axis=1, keepdims=True))
        scale = jnp.exp(old - new)
        weight = jnp.exp(logit - new)
        top[...] = new
        total[...] = total[...] * scale + jnp.sum(weight, axis=1, keepdims=True)
        weight_b = weight.astype(BF16)
        acc_single[...] = acc_single[...] * scale + mm(weight_b, single)
        vpoints = jnp.concatenate(placed(projected[2 * ROWS :], 96), axis=0)
        acc_points[...] = acc_points[...] * scale + nt(weight_b, vpoints)
        upper_rows = iota((GROUP, 128), 0) < 12
        for g in range(GROUPS):
            lo = g * GROUP
            there = jnp.concatenate(
                [
                    jnp.concatenate([pairs[2 * g, index] for index in pair_of], axis=0),
                    jnp.concatenate([pairs[2 * g + 1, index] for index in pair_of], axis=0),
                ],
                axis=1,
            )
            out = mm(weight[lo : lo + GROUP].astype(BF16), there)
            out = jnp.where(upper_rows, out[:, :128], out[:, 128:])
            acc_pair[g] = acc_pair[g] * scale[lo : lo + GROUP] + out
        return 0

    lax.fori_loop(0, 4, key_step, 0)

    inverse = 1.0 / total[...]
    row = iota((ROWS, 1), 0)
    query = by12(row)
    head = row - query * 12
    part_in[y, :ROWS] = (acc_pair[...].reshape(ROWS, 128) * inverse).astype(BF16)
    hi, lo = split2(acc_single[...] * inverse)
    scalar = nt(hi.astype(BF16), w_values[...]) + nt(lo.astype(BF16), w_values[...])
    scalar = jnp.where((iota((ROWS, ROWS), 1) >> 4) == head, scalar, 0.0).astype(BF16)
    lane = iota((1, 128), 1)
    again = lane & 63
    source = iota((ROWS, 128), 0)
    other = mm(scalar, ones_where(((source & 15) == again) & (again < 16)))
    center = centers[...]
    col = iota((1, 288), 1)
    axis = by96(col)
    center = jnp.where(axis == 0, center[:, :1], jnp.where(axis == 1, center[:, 1:2], center[:, 2:3]))
    shifted = jnp.where(((col - axis * 96) >> 3) == head, acc_points[...] * inverse - center, 0.0).astype(BF16)
    source = iota((288, 128), 0)
    other = other + mm(shifted, ones_where(again == by96(source) * 8 + (source & 7) + 16))
    for start, value in ((40, top[...]), (43, total[...])):
        for step, piece in enumerate(split3(value)):
            other = jnp.where(again == start + step, piece, other)
    half = ROWS // 2
    part_in[y, ROWS:] = jnp.where(lane < 64, other[:half], other[half:]).astype(BF16)

    parts_sent, parts_arriving = exchange(lambda peer: part_in.at[y], part_in, PART_OUT, PART_IN)
    for copy in parts_sent:
        copy.start()
    for copy in parts_arriving:
        copy.wait_recv()

    pair_parts = [part_in[k, :ROWS].astype(F32) for k in range(4)]
    others = []
    for k in range(4):
        both = part_in[k, ROWS:].astype(F32)
        others.append(jnp.concatenate([both, pltpu.roll(both, 64, 1)], axis=0))
    tops = [p[:, 40:41] + p[:, 41:42] + p[:, 42:43] for p in others]
    best = jnp.maximum(jnp.maximum(tops[0], tops[1]), jnp.maximum(tops[2], tops[3]))
    shares = [
        (p[:, 43:44] + p[:, 44:45] + p[:, 45:46]) * jnp.exp(t - best) for p, t in zip(others, tops)
    ]
    inverse = 1.0 / (shares[0] + shares[1] + shares[2] + shares[3])
    shares = [share * inverse for share in shares]
    o_pair = sum(p * s for p, s in zip(pair_parts, shares)).astype(BF16)
    other = sum(p * s for p, s in zip(others, shares))
    inside = (lane >= 16) & (lane < 40)
    point = lane & 7
    source = iota((128, 128), 0)
    first, second = split2(other)
    located = 0.0
    for b in range(3):
        pick = ones_where((source == point + 16 + 8 * b) & inside)
        located = located + turns[b] * (mm(first.astype(BF16), pick) + mm(second.astype(BF16), pick))
    last = (lane >= 40) & (lane < 48)
    pick = (source >= 16) & (source < 40) & ((source & 7) == point) & last
    first, second = split2(located * located)
    pick = ones_where(pick)
    length = jnp.sqrt(mm(first.astype(BF16), pick) + mm(second.astype(BF16), pick) + 1e-08)
    feats = jnp.where(lane < 16, other, jnp.where(inside, located, jnp.where(last, length, 0.0)))
    feats = jnp.concatenate([o_pair, feats.astype(BF16)], axis=1)
    row, col = iota((ROWS, ROWS), 0), iota((ROWS, ROWS), 1)
    query = by12(col)
    pick = ones_where(((row & 15) == query) & ((row >> 4) == col - query * 12))
    feats = mm(pick, feats).astype(BF16)
    out_copy.wait()
    update = v_single[...].astype(F32)
    for k in range(HEADS):
        here = feats[16 * k : 16 * k + 16]
        w = 176 * k
        update = update + mm(here[:, :128], v_wout[w + 16 : w + 144])
        rest = jnp.concatenate([v_wout[w : w + 16], v_wout[w + 144 : w + 176]], axis=0)
        update = update + mm(here[:, 128:176], rest)
    mixed_out[...] = update

    for name in EVENTS:
        for condition, copies, at_end in sends(name):
            if at_end:
                run(condition, copies, "wait_send")
    run(depth == 0, far_copies(1), "wait_send")
    for copy in rows_sent + weights_sent + parts_sent:
        copy.wait_send()


def finish(mixed_ref, gain, w_frame, frames, single_out, frames_out):
    mixed = mixed_ref[...]
    mean = jnp.mean(mixed, axis=1, keepdims=True)
    centered = mixed - mean
    var = jnp.mean(centered * centered, axis=1, keepdims=True)
    out = (centered / jnp.sqrt(var + 1e-05) * gain[...][None]).astype(BF16)
    single_out[...] = out
    shift = nt(w_frame[...], out)
    u = [shift[k : k + 1] for k in range(6)]
    length = jnp.sqrt(1.0 + u[0] * u[0] + u[1] * u[1] + u[2] * u[2])
    turn = quat_rotation(1.0 / length, u[0] / length, u[1] / length, u[2] / length)
    rot = [frames[k : k + 1] for k in range(12)]
    for a in range(3):
        for c in range(3):
            k = 3 * a + c
            frames_out[k : k + 1] = (
                rot[3 * a] * turn[c] + rot[3 * a + 1] * turn[3 + c] + rot[3 * a + 2] * turn[6 + c]
            )
        moved = rot[3 * a] * u[3] + rot[3 * a + 1] * u[4] + rot[3 * a + 2] * u[5]
        frames_out[9 + a : 10 + a] = moved + rot[9 + a]


def per_device(
    query_single, query_frames, query_chain, key_single, key_frames, key_chain, key_mask, pair,
    w_q, w_k, w_v, w_qp, w_kp, w_vp, w_bias, head_weight, chain_bias, w_out, ln_gain, w_frame,
):
    pair = pair.reshape(16, CHUNKS, KEYS, 128)
    vm = pltpu.VMEM
    anywhere = pl.BlockSpec(memory_space=pl.ANY)
    scalars = pl.BlockSpec(memory_space=pltpu.SMEM)
    inside = pl.BlockSpec(memory_space=pltpu.VMEM)
    mixed = pl.pallas_call(
        kernel,
        out_shape=jax.ShapeDtypeStruct((16, 384), F32),
        in_specs=[anywhere] * 16 + [scalars] * 2,
        out_specs=inside,
        scratch_shapes=[
            vm((16, 384), BF16), vm((12, 16), F32), vm((1, 16), jnp.int32), vm((12, 192), F32),
            vm((1, 192), jnp.int32), vm((1, 192), jnp.int32), vm((48, 384), BF16), vm((48, 384), BF16),
            vm((48, 384), BF16), vm((36, 384), BF16), vm((36, 384), BF16), vm((72, 384), BF16),
            vm((12, 128), BF16), vm((2112, 384), BF16),
            vm((16, CHUNKS, KEYS, 128), BF16), vm((CHUNKS, 2, 192, 384), BF16), vm((CHUNKS, 2, 16, 256), F32),
            vm((CHUNKS, GROUPS, GROUP, KEYS), F32), vm((4, 48, 512), BF16), vm((4, 176, 384), BF16),
            vm((2 * ROWS + 288, 384), BF16), vm((ROWS, 512), BF16), vm((ROWS, 384), BF16), vm((16, 1), F32),
            vm((32, 256), BF16),
            vm((GROUPS, GROUP, 128), F32), vm((ROWS, 384), F32), vm((ROWS, 288), F32),
            vm((ROWS, 1), F32), vm((ROWS, 1), F32), vm((4, 288, 128), BF16),
            vm((ROWS, 3), F32), vm((3, ROWS, 128), F32),
            pltpu.SemaphoreType.DMA((15,)), pltpu.SemaphoreType.DMA((GROUPS,)),
            pltpu.SemaphoreType.DMA((80,)), pltpu.SemaphoreType.DMA((64,)),
        ],
        compiler_params=pltpu.CompilerParams(
            collective_id=0, has_side_effects=True, vmem_limit_bytes=56 * 1024 * 1024
        ),
    )(
        query_single, query_frames, query_chain[None], key_single, key_frames, key_chain[None], key_mask[None], pair,
        w_q.T, w_k.T, w_v.T, w_qp.T, w_kp.T, w_vp.T, w_bias.T, w_out, head_weight, chain_bias,
    )
    return pl.pallas_call(
        finish,
        out_shape=(jax.ShapeDtypeStruct((16, 384), BF16), jax.ShapeDtypeStruct((12, 16), F32)),
        in_specs=[inside] * 4,
        out_specs=(inside, inside),
    )(mixed, ln_gain, w_frame.T, query_frames)


def solution(mesh):
    rows = ("sample", "blk")
    heads = P(None, "head")
    in_specs = (
        P(rows, None), P(None, rows), P(rows), P(rows, None), P(None, rows), P(rows), P(rows),
        P(rows, "head", None), heads, heads, heads, heads, heads, heads, P(), P("head"), P("head"),
        P(), P(), P(),
    )
    out_specs = (P(rows, None), P(None, rows))
    return jax.shard_map(
        per_device, mesh=mesh, in_specs=in_specs, out_specs=out_specs, check_vma=False
    )
```

```python
import math

import jax
import jax.numpy as jnp
from jax import lax
from jax.experimental import pallas as pl
from jax.experimental.pallas import tpu as pltpu
from jax.sharding import PartitionSpec as P

F32 = jnp.float32
BF16 = jnp.bfloat16
HIGH = lax.Precision.HIGHEST
MESH = pl.DeviceIdType.MESH

HEADS = 12
QPTS = 4
ROWS = 192
GROUPS = 8
GROUP = 24
EVENTS = {
    "z0": (0, 0, 0), "z1": (0, 1, 0), "l0": (1, 0, 0), "r0": (2, 0, 0), "z2": (0, 0, 1), "l1": (1, 1, 0),
    "r1": (2, 1, 0), "z3": (0, 1, 1), "l2": (1, 0, 1), "r2": (2, 0, 1), "l3": (1, 1, 1), "r3": (2, 1, 1),
    "o0": (3, 0, 1), "o1": (3, 1, 1),
}
SLOTS = {
    "z0": (-1, 3, 9), "z1": (3, 5, 9), "l0": (4, 9, 9), "r0": (4, 9, 9), "z2": (1, 8, 9), "l1": (9, 9, 9),
    "r1": (9, 9, 9), "z3": (8, 8, 9), "l2": (11, 11, 11), "r2": (11, 11, 11), "l3": (11, 11, 11),
    "r3": (11, 11, 11), "o0": (12, 12, 12), "o1": (13, 13, 13),
}
CHUNKS = 8
KEYS = 384
WEIGHT_L = math.sqrt(1.0 / 3.0)
WEIGHT_C = math.sqrt(2.0 / (9.0 * QPTS))

Z_IN, LEFT_IN, RIGHT_IN, HALF_LEFT_IN, HALF_RIGHT_IN, CORE_IN = 0, 4, 8, 12, 14, 16
ROWS_IN, WEIGHTS_IN, PART_IN, META = 24, 27, 30, 33
Z_OUT, Z_BACK, Z_LAST, RIGHT_OUT, LEFT_OUT, HALF_RIGHT_OUT, HALF_LEFT_OUT, CORE_OUT = 0, 4, 8, 12, 16, 20, 22, 24
ROWS_OUT, WEIGHTS_OUT, PART_OUT, META_OUT = 32, 35, 38, 41


def iota(shape, dim):
    return lax.broadcasted_iota(jnp.int32, shape, dim)


def by3(v):
    return (v * 171) >> 9


def by12(v):
    return (v * 171) >> 11


def by24(v):
    return (v * 2731) >> 16


def by48(v):
    return (v * 1366) >> 16


def by80(v):
    return (v * 820) >> 16


def by96(v):
    return (v * 683) >> 16


def ones_where(cond, dtype=BF16):
    return jnp.where(cond, 1.0, 0.0).astype(dtype)


def mm(lhs, rhs, precision=None):
    return lax.dot_general(
        lhs, rhs, (((1,), (0,)), ((), ())), precision=precision, preferred_element_type=F32
    )


def nt(lhs, rhs, precision=None):
    return lax.dot_general(
        lhs, rhs, (((1,), (1,)), ((), ())), precision=precision, preferred_element_type=F32
    )


def short(v):
    return v.astype(BF16).astype(F32)


def split2(v):
    first = short(v)
    return first, short(v - first)


def split3(v):
    first = short(v)
    second = short(v - first)
    return first, second, short(v - first - second)


def head16(head):
    owner = by3(head)
    return owner * 4 + head - owner * 3


def quat_rotation(w, x, y, z):
    return [
        1.0 - 2.0 * (y * y + z * z),
        2.0 * (x * y - w * z),
        2.0 * (x * z + w * y),
        2.0 * (x * y + w * z),
        1.0 - 2.0 * (x * x + z * z),
        2.0 * (y * z - w * x),
        2.0 * (x * z - w * y),
        2.0 * (y * z + w * x),
        1.0 - 2.0 * (x * x + y * y),
    ]


def own_rows(single, frames, chain, w_q, w_k, w_qp, head_weight, chain_bias):
    rows = 48
    row = iota((rows, 1), 0)
    query = by3(row)
    local_head = row - query * 3
    spread = query == iota((rows, 16), 1)
    single_rows = mm(ones_where(spread), single).astype(BF16)
    q_s = nt(single_rows, w_q).astype(BF16).astype(F32)
    col = iota((rows, 48), 1)
    q_s = jnp.where((col >> 4) == local_head, q_s, 0.0).astype(BF16)
    scalar = mm(q_s, w_k) * (WEIGHT_L / 4.0)

    frames = nt(ones_where(spread, F32), frames, HIGH)
    own_chain = jnp.sum(jnp.where(spread, chain.astype(F32), 0.0), axis=1, keepdims=True)
    local = nt(single_rows, w_qp)
    col = iota((rows, 36), 1)
    local = jnp.where(by12(col) == local_head, local, 0.0)
    lane = iota((1, 128), 1)
    comp = jnp.where(lane < 12, lane, lane - 12)
    axis = comp >> 2
    point = comp & 3
    inside = lane < 24
    source = iota((36, 128), 0)
    source = source - by12(source) * 12
    entry = iota((12, 128), 0)
    placed = mm(frames, ones_where((entry == axis + 9) & inside, F32), HIGH)
    for b in range(3):
        here = mm(local, ones_where((source == point + 4 * b) & inside, F32), HIGH)
        turn = mm(frames, ones_where((entry == axis * 3 + b) & inside, F32), HIGH)
        placed = placed + turn * here
    norm = jnp.sum(jnp.where(lane < 12, placed * placed, 0.0), axis=1, keepdims=True)

    def per_head(ref):
        return jnp.where(local_head == 0, ref[0], jnp.where(local_head == 1, ref[1], ref[2]))

    weight = per_head(head_weight)
    soft = jnp.maximum(weight, 0.0) + jnp.log(1.0 + jnp.exp(-jnp.abs(weight)))
    coeff = soft * (WEIGHT_L * WEIGHT_C / 2.0)
    point_hi, point_lo = split2(2.0 * coeff * placed)
    chain_hi, chain_lo = split2(per_head(chain_bias) * WEIGHT_L)
    lane_f = lane.astype(F32)
    compact = jnp.where(lane < 12, point_hi, jnp.where(inside, point_lo, 0.0))
    compact = jnp.where((lane >= 24) & (lane < 48) & (own_chain == lane_f - 24.0), chain_hi, compact)
    compact = jnp.where((lane >= 48) & (lane < 72) & (own_chain == lane_f - 48.0), chain_lo, compact)
    for first, values in ((72, split3(-coeff * norm)), (75, split3(coeff))):
        for step, value in enumerate(values):
            compact = jnp.where(lane == first + step, value, compact)
    return scalar.astype(BF16), compact.astype(BF16)


def own_weights(w_kp, w_v, w_vp):
    row = iota((48, 36), 0)
    col = iota((48, 36), 1)
    head = row & 3
    pick = (col == head * 12 + (row >> 4) * 4 + ((row >> 2) & 3)) & (head < 3)
    key_points = mm(ones_where(pick), w_kp).astype(BF16)
    row = iota((80, 72), 0)
    col = iota((80, 72), 1)
    b = by24(row)
    rest = row - b * 24
    pick = (col == (rest >> 3) * 24 + b * 8 + (rest & 7)) & (row < 72)
    value_points = mm(ones_where(pick), w_vp).astype(BF16)
    return key_points, w_v, value_points


def all_rows(packs):
    shape = (ROWS, ROWS)
    row, col = iota(shape, 0), iota(shape, 1)
    query = by12(row)
    owner = by48(col)
    rest = col - owner * 48
    col_query = by3(rest)
    pick = (query == col_query) & (row - query * 12 == owner * 3 + rest - col_query * 3)
    rows = mm(ones_where(pick), packs).astype(BF16)
    compact = rows[:, 384:]
    lane = iota((1, 512), 1)
    again = jnp.where(lane < 192, lane, lane - 192)
    source = ((again >> 6) * 4 + ((again >> 4) & 3)) + jnp.where(lane < 192, 0, 12)
    source = jnp.where(lane >= 384, -1, source)
    source = jnp.where((lane >= 384) & (lane < 408), lane - 360, source)
    source = jnp.where((lane >= 416) & (lane < 440), lane - 368, source)
    source = jnp.where((lane >= 496) & (lane < 499), lane - 424, source)
    other = mm(compact, ones_where(iota((128, 512), 0) == source))
    row = iota((ROWS, 1), 0)
    place = head16(row - by12(row) * 12)
    mine = (lane & 15) == place
    other = jnp.where(mine | (lane >= 384), other, 0.0)
    other = jnp.where(mine & (lane >= 448) & (lane < 496), 1.0, other)
    spot, col = iota((16, ROWS), 0), iota((16, ROWS), 1)
    pick = (head16(col) == spot) & (col < 12)
    factors = mm(ones_where(pick), compact)
    factor = factors[:, 75:76] + factors[:, 76:77] + factors[:, 77:78]
    return rows[:, :384], other.astype(BF16), factor


def kernel(
    single_q, frames_q, chain_q, single_k, frames_k, chain_k, mask_k, pair, w_q, w_k, w_v, w_qp, w_kp, w_vp, w_bias,
    w_out, head_weight, chain_bias,
    mixed_out,
    v_single, v_frames, v_chain, v_kframes, v_kchain, v_kmask, v_wq, v_wk, v_wv, v_wqp, v_wkp, v_wvp, v_wbias, v_wout,
    pairs, keys, metas, bias, pack_rows, pack_weights,
    projections, rows_other, w_values, factors, bias_rows,
    acc_pair, acc_single, acc_points, top, total, part_in, centers, turns,
    local_sem, pair_sem, send_sem, recv_sem,
):
    y = lax.axis_index("head")
    blk = lax.axis_index("blk")
    z = lax.div(blk, 8)
    core = lax.rem(blk, 2)
    x = lax.rem(lax.div(blk, 2), 4)
    r = lax.rem(z - 2 * y + 8, 8)
    upper = (r >= 1) & (r <= 4)
    depth = jnp.where(r <= 1, 0, jnp.where((r == 3) | (r == 6), 1, 2))
    near = jnp.where(upper, 1, 0)

    def device(zz, xx, cc):
        return (zz * 4 + xx) * 2 + cc

    partner = device(lax.rem(z + jnp.where(r == 0, 1, 7), 8), x, core)
    above, below = device(lax.rem(z + 1, 8), x, core), device(lax.rem(z + 7, 8), x, core)
    own_relay = device(lax.rem(2 * y + jnp.where(r == 1, 3, 6), 8), x, core)
    other_relay = device(lax.rem(2 * y + jnp.where(r == 1, 6, 3), 8), x, core)
    right = device(z, lax.rem(x + 1, 4), core)
    left = device(z, lax.rem(x + 3, 4), core)
    sibling = device(z, x, 1 - core)

    small = [
        (single_q, v_single), (frames_q, v_frames), (chain_q, v_chain), (w_q, v_wq), (w_k, v_wk), (w_qp, v_wqp),
        (w_kp, v_wkp), (w_v, v_wv), (w_vp, v_wvp), (w_bias, v_wbias),
    ]
    small = [pltpu.make_async_copy(src, dst, local_sem.at[i]) for i, (src, dst) in enumerate(small)]

    def item(phase, kind):
        plane = near if phase == 0 else 1 - near
        return plane * 4 + lax.rem(x + (0, 3, 1, 2)[kind], 4)

    def chunk_of(phase, kind):
        return (phase, 2 + 2 * phase, 3 + 2 * phase, 6 + phase)[kind]

    own_index = item(0, 0)
    own_copies = [
        pltpu.make_async_copy(src, dst, local_sem.at[10 + i])
        for i, (src, dst) in enumerate(
            ((frames_k, v_kframes), (chain_k, v_kchain), (mask_k, v_kmask), (single_k, keys.at[own_index, core]))
        )
    ]
    out_copy = pltpu.make_async_copy(w_out, v_wout, local_sem.at[14])
    pair_copies = [
        pltpu.make_async_copy(pair.at[pl.ds(2 * g, 2)], pairs.at[pl.ds(2 * g, 2)], pair_sem.at[g])
        for g in range(GROUPS)
    ]

    barrier = pltpu.get_barrier_semaphore()
    along_z = [(depth == 0, partner), (depth == 0, own_relay), (depth == 0, other_relay)]
    along_z += [(depth == 1, above), (depth == 1, below)]
    along_z += [(depth == 1, device(lax.rem(2 * y, 8), x, core)), (depth == 1, device(lax.rem(2 * y + 1, 8), x, core))]
    along_z += [(depth == 2, device(lax.rem(2 * y + jnp.where(upper, 3, 6), 8), x, core))]
    for condition, other in along_z:

        @pl.when(condition)
        def _(other=other):
            pl.semaphore_signal(barrier, inc=1, device_id={"blk": other}, device_id_type=MESH)

    for other in (right, left, sibling):
        pl.semaphore_signal(barrier, inc=1, device_id={"blk": other}, device_id_type=MESH)
    for step in (1, 2, 3):
        pl.semaphore_signal(
            barrier, inc=1, device_id={"head": lax.rem(y + step, 4)}, device_id_type=MESH
        )

    @pl.when(depth == 0)
    def _():
        for copy in own_copies:
            copy.start()

    for copy in small:
        copy.start()

    def remote(src, dst, sent, received, target):
        return pltpu.make_async_remote_copy(
            src_ref=src, dst_ref=dst, send_sem=send_sem.at[sent], recv_sem=recv_sem.at[received],
            device_id=target, device_id_type=MESH,
        )

    def block(index, cc, sent, received, target, half=None, meta=True, src=None):
        ref = keys.at[index, cc]
        if half is not None:
            ref = keys.at[index, cc, pl.ds(96 * half, 96)]
        copies = [remote(ref if src is None else src, ref, sent, received, {"blk": target})]
        if meta:
            ref = metas.at[index, cc]
            copies.append(remote(ref, ref, sent + META_OUT, received + META, {"blk": target}))
        return copies

    def sends(name):
        kind, phase, half = EVENTS[name]
        index = item(phase, kind)
        result = []
        step = 2 * phase + half
        meta = half == 0

        def add(condition, sent, received, target, at_end=True, src=None):
            result.append((condition, block(index, core, sent, received, target, half, meta, src), at_end))

        if kind == 0:
            if phase == 0:
                own = single_k.at[pl.ds(96 * half, 96)]
                add(depth == 0, Z_BACK + half, Z_IN + half, own_relay, False, own)
                add(depth == 0, Z_OUT + half, Z_IN + 2 + half, partner, True, own)
                add(depth == 0, RIGHT_OUT + step, LEFT_IN + step, right, True, own)
                add(depth == 0, LEFT_OUT + step, RIGHT_IN + step, left, True, own)
            add(depth == 1, Z_OUT + step, Z_IN + step, above)
            add(depth == 1, Z_BACK + step, Z_IN + step, below)
            passed = depth > 0 if phase == 0 else None
            add(passed, RIGHT_OUT + step, LEFT_IN + step, right)
            add(passed, LEFT_OUT + step, RIGHT_IN + step, left)
        if kind == 1 and half == 0:
            add(None, HALF_RIGHT_OUT + phase, HALF_LEFT_IN + phase, right)
        if kind == 2 and half == 1:
            add(None, HALF_LEFT_OUT + phase, HALF_RIGHT_IN + phase, left)
        if half == 1:
            i = chunk_of(phase, kind)
            result.append((None, block(index, core, CORE_OUT + i, CORE_IN + i, sibling), True))
        return result

    def near_copies(half):
        own = single_k.at[pl.ds(96 * half, 96)]
        return block(own_index, core, Z_BACK + half, Z_IN + half, own_relay, half, half == 0, own)

    def far_copies(half):
        own = single_k.at[pl.ds(96 * half, 96)]
        return block(own_index, core, Z_LAST + half, Z_IN + 2 + half, other_relay, half, half == 0, own)

    def run(condition, copies, verb):
        def act():
            for copy in copies:
                getattr(copy, verb)()

        if condition is None:
            act()
        else:
            pl.when(condition)(act)

    def event(name):
        kind, phase, half = EVENTS[name]
        index = item(phase, kind)
        step = 2 * phase + half
        if kind == 3:
            arriving = block(index, core, 0, HALF_LEFT_IN + phase, sibling, 0)
            arriving += block(index, core, 0, HALF_RIGHT_IN + phase, sibling, 1, False)
        else:
            place = (Z_IN, LEFT_IN, RIGHT_IN)[kind] + step
            arriving = block(index, core, 0, place, sibling, half, half == 0)
        run(depth > 0 if kind == 0 and phase == 0 else None, arriving, "wait_recv")
        for condition, copies, _ in sends(name):
            run(condition, copies, "start")

    slots = {
        name: jnp.where(depth == 0, when[0], jnp.where(depth == 1, when[1], when[2])) for name, when in SLOTS.items()
    }

    def events_at(step, names):
        for name in names:
            pl.when(slots[name] == step)(lambda name=name: event(name))

    pl.semaphore_wait(barrier, jnp.where(depth == 0, 9, jnp.where(depth == 1, 10, 7)))
    first = [copies for condition, copies, _ in sends("z0") if condition is not None][:4]

    @pl.when(depth == 0)
    def _():
        for copies in first:
            copies[0].start()
        for copy in own_copies[:3]:
            copy.wait()
        metas[own_index, core] = jnp.zeros((16, 256), F32)
        metas[own_index, core, :12, :192] = v_kframes[...]
        metas[own_index, core, 12:13, :192] = v_kchain[...].astype(F32)
        metas[own_index, core, 13:14, :192] = v_kmask[...].astype(F32)
        for copies in first:
            copies[1].start()

    for copy in pair_copies:
        copy.start()
    out_copy.start()

    for copy in small:
        copy.wait()
    scalar, compact = own_rows(
        v_single[...], v_frames[...], v_chain[...], v_wq[...], v_wk[...], v_wqp[...], head_weight, chain_bias
    )
    pack_rows[y, :, :384] = scalar
    pack_rows[y, :, 384:] = compact
    key_points, values, value_points = own_weights(v_wkp[...], v_wv[...], v_wvp[...])
    pack_weights[y, :48] = key_points
    pack_weights[y, 48:96] = values
    pack_weights[y, 96:] = value_points

    def exchange(src, dst, sent, received):
        out, arriving = [], []
        for step in (1, 2, 3):
            peer = lax.rem(y + step, 4)
            origin = lax.rem(y + 4 - step, 4)
            out.append(remote(src(peer), dst.at[y], sent + step - 1, received + step - 1, {"head": peer}))
            arriving.append(
                remote(dst.at[origin], dst.at[origin], sent + step - 1, received + step - 1, {"head": peer})
            )
        return out, arriving

    rows_sent, rows_arriving = exchange(lambda peer: pack_rows.at[y], pack_rows, ROWS_OUT, ROWS_IN)
    weights_sent, weights_arriving = exchange(
        lambda peer: pack_weights.at[y], pack_weights, WEIGHTS_OUT, WEIGHTS_IN
    )
    for copy in rows_sent + weights_sent:
        copy.start()

    row = iota((ROWS, 16), 0)
    frames = nt(ones_where(by12(row) == iota((ROWS, 16), 1), F32), v_frames[...], HIGH)
    centers[...] = frames[:, 9:12]
    lane = iota((1, 128), 1)
    axis = (lane - 16) >> 3
    inside = (lane >= 16) & (lane < 40)
    entry = iota((12, 128), 0)
    for b in range(3):
        turns[b] = mm(frames, ones_where((entry == 3 * b + axis) & inside, F32), HIGH)

    run(depth == 0, near_copies(0), "wait_send")
    run(depth == 0, far_copies(0), "start")

    col = iota((32, 12), 1)
    pick_row = iota((32, 12), 0)
    first = mm(ones_where(pick_row == col), v_wbias[...])
    second = mm(ones_where(pick_row == col + 12), v_wbias[...])
    bias_rows[:, :128] = first.astype(BF16)
    bias_rows[:, 128:] = second.astype(BF16)

    def bias_step(t, _):
        pltpu.make_async_copy(pair.at[pl.ds(2 * t, 2)], pairs.at[pl.ds(2 * t, 2)], pair_sem.at[t]).wait()
        for c in range(0, CHUNKS, 2):
            block_a = pairs[2 * t, c : c + 2].reshape(2 * KEYS, 128)
            block_b = pairs[2 * t + 1, c : c + 2].reshape(2 * KEYS, 128)
            out = nt(bias_rows[...], jnp.concatenate([block_a, block_b], axis=1))[:GROUP]
            out = short(out) * WEIGHT_L
            bias[c, t] = out[:, :KEYS]
            bias[c + 1, t] = out[:, KEYS:]
        run((depth == 0) & (t == 1), far_copies(0), "wait_send")
        run((depth == 0) & (t == 3), near_copies(1), "wait_send")
        run((depth == 0) & (t == 3), far_copies(1), "start")
        run((depth == 0) & (t == 1), own_copies[3:], "wait")
        events_at(t, [name for name, when in SLOTS.items() if any(0 <= k < 8 for k in when)])
        return 0

    lax.fori_loop(0, GROUPS, bias_step, 0)
    events_at(8, ["z2", "z3"])
    events_at(9, [name for name, when in SLOTS.items() if 9 in when])

    for copy in rows_arriving + weights_arriving:
        copy.wait_recv()
    for_single, for_other, factor = all_rows(pack_rows[...].reshape(ROWS, 512))
    projections[:ROWS] = for_single
    rows_other[...] = for_other
    factors[...] = -factor
    packs = pack_weights[...]
    row, col = iota((ROWS, ROWS), 0), iota((ROWS, ROWS), 1)
    place = row & 15
    pick = col == (place >> 2) * 48 + (row >> 6) * 16 + ((row >> 4) & 3) * 4 + (place & 3)
    projections[ROWS : 2 * ROWS] = mm(ones_where(pick), packs[:, :48].reshape(ROWS, 384)).astype(BF16)
    w_values[...] = packs[:, 48:96].reshape(ROWS, 384)
    row, col = iota((288, 320), 0), iota((288, 320), 1)
    b = by96(row)
    rest = row - b * 96
    owner = by24(rest)
    pick = col == owner * 80 + b * 24 + rest - owner * 24
    projections[2 * ROWS :] = mm(ones_where(pick), packs[:, 96:].reshape(320, 384)).astype(BF16)

    acc_pair[...] = jnp.zeros_like(acc_pair)
    acc_single[...] = jnp.zeros_like(acc_single)
    acc_points[...] = jnp.zeros_like(acc_points)
    top[...] = jnp.full_like(top, -1e30)
    total[...] = jnp.zeros_like(total)

    indices = [item(*pair) for pair in ((0, 0), (1, 0), (0, 1), (0, 2), (1, 1), (1, 2), (0, 3), (1, 3))]

    def index_of(i):
        value = indices[7]
        for k in range(7):
            value = jnp.where(i == k, indices[k], value)
        return value

    def key_meta(index):
        half = iota((16, 128), 1) < 64
        first, second = metas[index, 0], metas[index, 1]
        start = pltpu.roll(second[:, :128], 64, 1)
        end = pltpu.roll(second[:, 128:], 64, 1)
        return [first[:, :128], jnp.where(half, first[:, 128:], start), jnp.where(half, start, end)]

    def front(s):
        pair_of = [index_of(2 * s), index_of(2 * s + 1)]
        for k, index in enumerate(pair_of):
            i = 2 * s + k
            here = keys.at[index, 1 - core]
            remote(here, here, 0, CORE_IN + i, {"blk": sibling}).wait_recv()
            here = metas.at[index, 1 - core]
            remote(here, here, 0, META + CORE_IN + i, {"blk": sibling}).wait_recv()

        single = jnp.concatenate([keys[index].reshape(KEYS, 384) for index in pair_of], axis=0)
        meta = jnp.concatenate(key_meta(pair_of[0]) + key_meta(pair_of[1]), axis=1)

        def placed(local, rows):
            result = []
            for a in range(3):
                moved = meta[9 + a : 10 + a] + meta[3 * a : 3 * a + 1] * local[:rows]
                moved = moved + meta[3 * a + 1 : 3 * a + 2] * local[rows : 2 * rows]
                moved = moved + meta[3 * a + 2 : 3 * a + 3] * local[2 * rows :]
                result.append(moved.astype(BF16))
            return result

        projected = nt(projections[...], single)
        points = placed(projected[ROWS : 2 * ROWS], 64)
        square = 0.0
        for part in points:
            wide = part.astype(F32)
            square = square + wide * wide
        norm = square[:16] + square[16:32] + square[32:48] + square[48:]
        norms = [v.astype(BF16) for v in split3(norm * factors[...])]
        width = 2 * KEYS
        chains = ones_where(meta[12:13] == iota((32, width), 0).astype(F32))
        others = jnp.concatenate(
            points + points + [chains, chains] + norms + [jnp.full((16, width), 1.0, BF16)], axis=0
        )
        logit = projected[:ROWS] + mm(rows_other[...], others)
        logit = logit + jnp.concatenate([bias[index].reshape(ROWS, KEYS) for index in pair_of], axis=1)
        logit = jnp.where(meta[13:14] > 0.5, logit, -1000000000.0)
        vpoints = jnp.concatenate(placed(projected[2 * ROWS :], 96), axis=0)
        return logit, vpoints

    def back(s, logit, vpoints):
        pair_of = [index_of(2 * s), index_of(2 * s + 1)]
        single = jnp.concatenate([keys[index].reshape(KEYS, 384) for index in pair_of], axis=0)
        old = top[...]
        new = jnp.maximum(old, jnp.max(logit, axis=1, keepdims=True))
        scale = jnp.exp(old - new)
        weight = jnp.exp(logit - new)
        top[...] = new
        total[...] = total[...] * scale + jnp.sum(weight, axis=1, keepdims=True)
        weight_b = weight.astype(BF16)
        acc_single[...] = acc_single[...] * scale + mm(weight_b, single)
        acc_points[...] = acc_points[...] * scale + nt(weight_b, vpoints)
        upper_rows = iota((GROUP, 128), 0) < 12
        for g in range(GROUPS):
            lo = g * GROUP
            there = jnp.concatenate(
                [
                    jnp.concatenate([pairs[2 * g, index] for index in pair_of], axis=0),
                    jnp.concatenate([pairs[2 * g + 1, index] for index in pair_of], axis=0),
                ],
                axis=1,
            )
            out = mm(weight[lo : lo + GROUP].astype(BF16), there)
            out = jnp.where(upper_rows, out[:, :128], out[:, 128:])
            acc_pair[g] = acc_pair[g] * scale[lo : lo + GROUP] + out

    def key_step(s, before):
        events_at(s + 10, [name for name, when in SLOTS.items() if max(when) > 9])
        after = front(s)
        back(s - 1, *before)
        return after

    back(3, *lax.fori_loop(1, 4, key_step, front(0)))

    inverse = 1.0 / total[...]
    row = iota((ROWS, 1), 0)
    query = by12(row)
    head = row - query * 12
    part_in[y, :ROWS] = (acc_pair[...].reshape(ROWS, 128) * inverse).astype(BF16)
    hi, lo = split2(acc_single[...] * inverse)
    scalar = nt(hi.astype(BF16), w_values[...]) + nt(lo.astype(BF16), w_values[...])
    scalar = jnp.where((iota((ROWS, ROWS), 1) >> 4) == head, scalar, 0.0).astype(BF16)
    lane = iota((1, 128), 1)
    again = lane & 63
    source = iota((ROWS, 128), 0)
    other = mm(scalar, ones_where(((source & 15) == again) & (again < 16)))
    center = centers[...]
    col = iota((1, 288), 1)
    axis = by96(col)
    center = jnp.where(axis == 0, center[:, :1], jnp.where(axis == 1, center[:, 1:2], center[:, 2:3]))
    shifted = jnp.where(((col - axis * 96) >> 3) == head, acc_points[...] * inverse - center, 0.0).astype(BF16)
    source = iota((288, 128), 0)
    other = other + mm(shifted, ones_where(again == by96(source) * 8 + (source & 7) + 16))
    for start, value in ((40, top[...]), (43, total[...])):
        for step, piece in enumerate(split3(value)):
            other = jnp.where(again == start + step, piece, other)
    half = ROWS // 2
    part_in[y, ROWS:] = jnp.where(lane < 64, other[:half], other[half:]).astype(BF16)

    parts_sent, parts_arriving = exchange(lambda peer: part_in.at[y], part_in, PART_OUT, PART_IN)
    for copy in parts_sent:
        copy.start()
    for copy in parts_arriving:
        copy.wait_recv()

    pair_parts = [part_in[k, :ROWS].astype(F32) for k in range(4)]
    others = []
    for k in range(4):
        both = part_in[k, ROWS:].astype(F32)
        others.append(jnp.concatenate([both, pltpu.roll(both, 64, 1)], axis=0))
    tops = [p[:, 40:41] + p[:, 41:42] + p[:, 42:43] for p in others]
    best = jnp.maximum(jnp.maximum(tops[0], tops[1]), jnp.maximum(tops[2], tops[3]))
    shares = [
        (p[:, 43:44] + p[:, 44:45] + p[:, 45:46]) * jnp.exp(t - best) for p, t in zip(others, tops)
    ]
    inverse = 1.0 / (shares[0] + shares[1] + shares[2] + shares[3])
    shares = [share * inverse for share in shares]
    o_pair = sum(p * s for p, s in zip(pair_parts, shares)).astype(BF16)
    other = sum(p * s for p, s in zip(others, shares))
    inside = (lane >= 16) & (lane < 40)
    point = lane & 7
    source = iota((128, 128), 0)
    first, second = split2(other)
    located = 0.0
    for b in range(3):
        pick = ones_where((source == point + 16 + 8 * b) & inside)
        located = located + turns[b] * (mm(first.astype(BF16), pick) + mm(second.astype(BF16), pick))
    last = (lane >= 40) & (lane < 48)
    pick = (source >= 16) & (source < 40) & ((source & 7) == point) & last
    first, second = split2(located * located)
    pick = ones_where(pick)
    length = jnp.sqrt(mm(first.astype(BF16), pick) + mm(second.astype(BF16), pick) + 1e-08)
    feats = jnp.where(lane < 16, other, jnp.where(inside, located, jnp.where(last, length, 0.0)))
    feats = jnp.concatenate([o_pair, feats.astype(BF16)], axis=1)
    row, col = iota((ROWS, ROWS), 0), iota((ROWS, ROWS), 1)
    query = by12(col)
    pick = ones_where(((row & 15) == query) & ((row >> 4) == col - query * 12))
    feats = mm(pick, feats).astype(BF16)
    out_copy.wait()
    update = v_single[...].astype(F32)
    for k in range(HEADS):
        here = feats[16 * k : 16 * k + 16]
        w = 176 * k
        update = update + mm(here[:, :128], v_wout[w + 16 : w + 144])
        rest = jnp.concatenate([v_wout[w : w + 16], v_wout[w + 144 : w + 176]], axis=0)
        update = update + mm(here[:, 128:176], rest)
    mixed_out[...] = update

    for name in EVENTS:
        for condition, copies, at_end in sends(name):
            if at_end:
                run(condition, copies, "wait_send")
    run(depth == 0, far_copies(1), "wait_send")
    for copy in rows_sent + weights_sent + parts_sent:
        copy.wait_send()


def finish(mixed_ref, gain, w_frame, frames, single_out, frames_out):
    mixed = mixed_ref[...]
    mean = jnp.mean(mixed, axis=1, keepdims=True)
    centered = mixed - mean
    var = jnp.mean(centered * centered, axis=1, keepdims=True)
    out = (centered / jnp.sqrt(var + 1e-05) * gain[...][None]).astype(BF16)
    single_out[...] = out
    shift = nt(w_frame[...], out)
    u = [shift[k : k + 1] for k in range(6)]
    length = jnp.sqrt(1.0 + u[0] * u[0] + u[1] * u[1] + u[2] * u[2])
    turn = quat_rotation(1.0 / length, u[0] / length, u[1] / length, u[2] / length)
    rot = [frames[k : k + 1] for k in range(12)]
    for a in range(3):
        for c in range(3):
            k = 3 * a + c
            frames_out[k : k + 1] = (
                rot[3 * a] * turn[c] + rot[3 * a + 1] * turn[3 + c] + rot[3 * a + 2] * turn[6 + c]
            )
        moved = rot[3 * a] * u[3] + rot[3 * a + 1] * u[4] + rot[3 * a + 2] * u[5]
        frames_out[9 + a : 10 + a] = moved + rot[9 + a]


def per_device(
    query_single, query_frames, query_chain, key_single, key_frames, key_chain, key_mask, pair,
    w_q, w_k, w_v, w_qp, w_kp, w_vp, w_bias, head_weight, chain_bias, w_out, ln_gain, w_frame,
):
    pair = pair.reshape(16, CHUNKS, KEYS, 128)
    vm = pltpu.VMEM
    anywhere = pl.BlockSpec(memory_space=pl.ANY)
    scalars = pl.BlockSpec(memory_space=pltpu.SMEM)
    inside = pl.BlockSpec(memory_space=pltpu.VMEM)
    mixed = pl.pallas_call(
        kernel,
        out_shape=jax.ShapeDtypeStruct((16, 384), F32),
        in_specs=[anywhere] * 16 + [scalars] * 2,
        out_specs=inside,
        scratch_shapes=[
            vm((16, 384), BF16), vm((12, 16), F32), vm((1, 16), jnp.int32), vm((12, 192), F32),
            vm((1, 192), jnp.int32), vm((1, 192), jnp.int32), vm((48, 384), BF16), vm((48, 384), BF16),
            vm((48, 384), BF16), vm((36, 384), BF16), vm((36, 384), BF16), vm((72, 384), BF16),
            vm((12, 128), BF16), vm((2112, 384), BF16),
            vm((16, CHUNKS, KEYS, 128), BF16), vm((CHUNKS, 2, 192, 384), BF16), vm((CHUNKS, 2, 16, 256), F32),
            vm((CHUNKS, GROUPS, GROUP, KEYS), F32), vm((4, 48, 512), BF16), vm((4, 176, 384), BF16),
            vm((2 * ROWS + 288, 384), BF16), vm((ROWS, 512), BF16), vm((ROWS, 384), BF16), vm((16, 1), F32),
            vm((32, 256), BF16),
            vm((GROUPS, GROUP, 128), F32), vm((ROWS, 384), F32), vm((ROWS, 288), F32),
            vm((ROWS, 1), F32), vm((ROWS, 1), F32), vm((4, 288, 128), BF16),
            vm((ROWS, 3), F32), vm((3, ROWS, 128), F32),
            pltpu.SemaphoreType.DMA((15,)), pltpu.SemaphoreType.DMA((GROUPS,)),
            pltpu.SemaphoreType.DMA((80,)), pltpu.SemaphoreType.DMA((64,)),
        ],
        compiler_params=pltpu.CompilerParams(
            collective_id=0, has_side_effects=True, vmem_limit_bytes=56 * 1024 * 1024
        ),
    )(
        query_single, query_frames, query_chain[None], key_single, key_frames, key_chain[None], key_mask[None], pair,
        w_q.T, w_k.T, w_v.T, w_qp.T, w_kp.T, w_vp.T, w_bias.T, w_out, head_weight, chain_bias,
    )
    return pl.pallas_call(
        finish,
        out_shape=(jax.ShapeDtypeStruct((16, 384), BF16), jax.ShapeDtypeStruct((12, 16), F32)),
        in_specs=[inside] * 4,
        out_specs=(inside, inside),
    )(mixed, ln_gain, w_frame.T, query_frames)


def solution(mesh):
    rows = ("sample", "blk")
    heads = P(None, "head")
    in_specs = (
        P(rows, None), P(None, rows), P(rows), P(rows, None), P(None, rows), P(rows), P(rows),
        P(rows, "head", None), heads, heads, heads, heads, heads, heads, P(), P("head"), P("head"),
        P(), P(), P(),
    )
    out_specs = (P(rows, None), P(None, rows))
    return jax.shard_map(
        per_device, mesh=mesh, in_specs=in_specs, out_specs=out_specs, check_vma=False
    )
```

```python
import math

import jax
import jax.numpy as jnp
from jax import lax
from jax.experimental import pallas as pl
from jax.experimental.pallas import tpu as pltpu
from jax.sharding import PartitionSpec as P

F32 = jnp.float32
BF16 = jnp.bfloat16
HIGH = lax.Precision.HIGHEST
MESH = pl.DeviceIdType.MESH

HEADS = 12
QPTS = 4
ROWS = 192
GROUPS = 8
GROUP = 24
EVENTS = {
    "z0": (0, 0, 0), "z1": (0, 1, 0), "l0": (1, 0, 0), "r0": (2, 0, 0), "z2": (0, 0, 1), "l1": (1, 1, 0),
    "r1": (2, 1, 0), "z3": (0, 1, 1), "l2": (1, 0, 1), "r2": (2, 0, 1), "l3": (1, 1, 1), "r3": (2, 1, 1),
    "o0": (3, 0, 1), "o1": (3, 1, 1),
}
SLOTS = {
    "z0": (-1, 3, 9), "z1": (3, 5, 9), "l0": (4, 9, 9), "r0": (4, 9, 9), "z2": (1, 8, 9), "l1": (9, 9, 9),
    "r1": (9, 9, 9), "z3": (8, 8, 9), "l2": (11, 11, 11), "r2": (11, 11, 11), "l3": (11, 11, 11),
    "r3": (11, 11, 11), "o0": (12, 12, 12), "o1": (13, 13, 13),
}
CHUNKS = 8
KEYS = 384
WEIGHT_L = math.sqrt(1.0 / 3.0)
WEIGHT_C = math.sqrt(2.0 / (9.0 * QPTS))

Z_IN, LEFT_IN, RIGHT_IN, HALF_LEFT_IN, HALF_RIGHT_IN, CORE_IN = 0, 4, 8, 12, 14, 16
ROWS_IN, WEIGHTS_IN, PART_IN, META, REST_IN = 24, 27, 30, 33, 57
Z_OUT, Z_BACK, Z_LAST, RIGHT_OUT, LEFT_OUT, HALF_RIGHT_OUT, HALF_LEFT_OUT, CORE_OUT = 0, 4, 8, 12, 16, 20, 22, 24
ROWS_OUT, WEIGHTS_OUT, PART_OUT, META_OUT, REST_OUT = 32, 35, 38, 41, 74


def iota(shape, dim):
    return lax.broadcasted_iota(jnp.int32, shape, dim)


def by3(v):
    return (v * 171) >> 9


def by12(v):
    return (v * 171) >> 11


def by24(v):
    return (v * 2731) >> 16


def by48(v):
    return (v * 1366) >> 16


def by80(v):
    return (v * 820) >> 16


def by96(v):
    return (v * 683) >> 16


def ones_where(cond, dtype=BF16):
    return jnp.where(cond, 1.0, 0.0).astype(dtype)


def mm(lhs, rhs, precision=None):
    return lax.dot_general(
        lhs, rhs, (((1,), (0,)), ((), ())), precision=precision, preferred_element_type=F32
    )


def nt(lhs, rhs, precision=None):
    return lax.dot_general(
        lhs, rhs, (((1,), (1,)), ((), ())), precision=precision, preferred_element_type=F32
    )


def short(v):
    return v.astype(BF16).astype(F32)


def split2(v):
    first = short(v)
    return first, short(v - first)


def split3(v):
    first = short(v)
    second = short(v - first)
    return first, second, short(v - first - second)


def head16(head):
    owner = by3(head)
    return owner * 4 + head - owner * 3


def quat_rotation(w, x, y, z):
    return [
        1.0 - 2.0 * (y * y + z * z),
        2.0 * (x * y - w * z),
        2.0 * (x * z + w * y),
        2.0 * (x * y + w * z),
        1.0 - 2.0 * (x * x + z * z),
        2.0 * (y * z - w * x),
        2.0 * (x * z - w * y),
        2.0 * (y * z + w * x),
        1.0 - 2.0 * (x * x + y * y),
    ]


def own_rows(single, frames, chain, w_q, w_k, w_qp, head_weight, chain_bias):
    rows = 48
    row = iota((rows, 1), 0)
    query = by3(row)
    local_head = row - query * 3
    spread = query == iota((rows, 16), 1)
    single_rows = mm(ones_where(spread), single).astype(BF16)
    q_s = nt(single_rows, w_q).astype(BF16).astype(F32)
    col = iota((rows, 48), 1)
    q_s = jnp.where((col >> 4) == local_head, q_s, 0.0).astype(BF16)
    scalar = mm(q_s, w_k) * (WEIGHT_L / 4.0)

    frames = nt(ones_where(spread, F32), frames, HIGH)
    own_chain = jnp.sum(jnp.where(spread, chain.astype(F32), 0.0), axis=1, keepdims=True)
    local = nt(single_rows, w_qp)
    col = iota((rows, 36), 1)
    local = jnp.where(by12(col) == local_head, local, 0.0)
    lane = iota((1, 128), 1)
    comp = jnp.where(lane < 12, lane, lane - 12)
    axis = comp >> 2
    point = comp & 3
    inside = lane < 24
    source = iota((36, 128), 0)
    source = source - by12(source) * 12
    entry = iota((12, 128), 0)
    placed = mm(frames, ones_where((entry == axis + 9) & inside, F32), HIGH)
    for b in range(3):
        here = mm(local, ones_where((source == point + 4 * b) & inside, F32), HIGH)
        turn = mm(frames, ones_where((entry == axis * 3 + b) & inside, F32), HIGH)
        placed = placed + turn * here
    norm = jnp.sum(jnp.where(lane < 12, placed * placed, 0.0), axis=1, keepdims=True)

    def per_head(ref):
        return jnp.where(local_head == 0, ref[0], jnp.where(local_head == 1, ref[1], ref[2]))

    weight = per_head(head_weight)
    soft = jnp.maximum(weight, 0.0) + jnp.log(1.0 + jnp.exp(-jnp.abs(weight)))
    coeff = soft * (WEIGHT_L * WEIGHT_C / 2.0)
    point_hi, point_lo = split2(2.0 * coeff * placed)
    chain_hi, chain_lo = split2(per_head(chain_bias) * WEIGHT_L)
    lane_f = lane.astype(F32)
    compact = jnp.where(lane < 12, point_hi, jnp.where(inside, point_lo, 0.0))
    compact = jnp.where((lane >= 24) & (lane < 48) & (own_chain == lane_f - 24.0), chain_hi, compact)
    compact = jnp.where((lane >= 48) & (lane < 72) & (own_chain == lane_f - 48.0), chain_lo, compact)
    for first, values in ((72, split3(-coeff * norm)), (75, split3(coeff))):
        for step, value in enumerate(values):
            compact = jnp.where(lane == first + step, value, compact)
    return scalar.astype(BF16), compact.astype(BF16)


def own_weights(w_kp, w_v, w_vp):
    row = iota((48, 36), 0)
    col = iota((48, 36), 1)
    head = row & 3
    pick = (col == head * 12 + (row >> 4) * 4 + ((row >> 2) & 3)) & (head < 3)
    key_points = mm(ones_where(pick), w_kp).astype(BF16)
    row = iota((80, 72), 0)
    col = iota((80, 72), 1)
    b = by24(row)
    rest = row - b * 24
    pick = (col == (rest >> 3) * 24 + b * 8 + (rest & 7)) & (row < 72)
    value_points = mm(ones_where(pick), w_vp).astype(BF16)
    return key_points, w_v, value_points


def all_rows(packs):
    shape = (ROWS, ROWS)
    row, col = iota(shape, 0), iota(shape, 1)
    query = by12(row)
    owner = by48(col)
    rest = col - owner * 48
    col_query = by3(rest)
    pick = (query == col_query) & (row - query * 12 == owner * 3 + rest - col_query * 3)
    rows = mm(ones_where(pick), packs).astype(BF16)
    compact = rows[:, 384:]
    lane = iota((1, 512), 1)
    again = jnp.where(lane < 192, lane, lane - 192)
    source = ((again >> 6) * 4 + ((again >> 4) & 3)) + jnp.where(lane < 192, 0, 12)
    source = jnp.where(lane >= 384, -1, source)
    source = jnp.where((lane >= 384) & (lane < 408), lane - 360, source)
    source = jnp.where((lane >= 416) & (lane < 440), lane - 368, source)
    source = jnp.where((lane >= 496) & (lane < 499), lane - 424, source)
    other = mm(compact, ones_where(iota((128, 512), 0) == source))
    row = iota((ROWS, 1), 0)
    place = head16(row - by12(row) * 12)
    mine = (lane & 15) == place
    other = jnp.where(mine | (lane >= 384), other, 0.0)
    other = jnp.where(mine & (lane >= 448) & (lane < 496), 1.0, other)
    spot, col = iota((16, ROWS), 0), iota((16, ROWS), 1)
    pick = (head16(col) == spot) & (col < 12)
    factors = mm(ones_where(pick), compact)
    factor = factors[:, 75:76] + factors[:, 76:77] + factors[:, 77:78]
    return rows[:, :384], other.astype(BF16), factor


def kernel(
    single_q, frames_q, chain_q, single_k, frames_k, chain_k, mask_k, pair, w_q, w_k, w_v, w_qp, w_kp, w_vp, w_bias,
    w_out, head_weight, chain_bias,
    mixed_out,
    v_single, v_frames, v_chain, v_kframes, v_kchain, v_kmask, v_wq, v_wk, v_wv, v_wqp, v_wkp, v_wvp, v_wbias, v_wout,
    pairs, keys, metas, bias, pack_rows, pack_weights,
    projections, rows_other, w_values, factors, bias_rows,
    acc_pair, acc_single, acc_points, top, total, part_in, rest_in, centers, turns,
    local_sem, pair_sem, send_sem, recv_sem,
):
    y = lax.axis_index("head")
    blk = lax.axis_index("blk")
    z = lax.div(blk, 8)
    core = lax.rem(blk, 2)
    x = lax.rem(lax.div(blk, 2), 4)
    r = lax.rem(z - 2 * y + 8, 8)
    upper = (r >= 1) & (r <= 4)
    depth = jnp.where(r <= 1, 0, jnp.where((r == 3) | (r == 6), 1, 2))
    near = jnp.where(upper, 1, 0)

    def device(zz, xx, cc):
        return (zz * 4 + xx) * 2 + cc

    partner = device(lax.rem(z + jnp.where(r == 0, 1, 7), 8), x, core)
    above, below = device(lax.rem(z + 1, 8), x, core), device(lax.rem(z + 7, 8), x, core)
    own_relay = device(lax.rem(2 * y + jnp.where(r == 1, 3, 6), 8), x, core)
    other_relay = device(lax.rem(2 * y + jnp.where(r == 1, 6, 3), 8), x, core)
    right = device(z, lax.rem(x + 1, 4), core)
    left = device(z, lax.rem(x + 3, 4), core)
    sibling = device(z, x, 1 - core)

    small = [
        (single_q, v_single), (frames_q, v_frames), (chain_q, v_chain), (w_q, v_wq), (w_k, v_wk), (w_qp, v_wqp),
        (w_kp, v_wkp), (w_v, v_wv), (w_vp, v_wvp), (w_bias, v_wbias),
    ]
    small = [pltpu.make_async_copy(src, dst, local_sem.at[i]) for i, (src, dst) in enumerate(small)]

    def item(phase, kind):
        plane = near if phase == 0 else 1 - near
        return plane * 4 + lax.rem(x + (0, 3, 1, 2)[kind], 4)

    def chunk_of(phase, kind):
        return (phase, 2 + 2 * phase, 3 + 2 * phase, 6 + phase)[kind]

    own_index = item(0, 0)
    own_copies = [
        pltpu.make_async_copy(src, dst, local_sem.at[10 + i])
        for i, (src, dst) in enumerate(
            ((frames_k, v_kframes), (chain_k, v_kchain), (mask_k, v_kmask), (single_k, keys.at[own_index, core]))
        )
    ]
    out_copy = pltpu.make_async_copy(w_out, v_wout, local_sem.at[14])
    pair_copies = [
        pltpu.make_async_copy(pair.at[pl.ds(2 * g, 2)], pairs.at[pl.ds(2 * g, 2)], pair_sem.at[g])
        for g in range(GROUPS)
    ]

    barrier = pltpu.get_barrier_semaphore()
    along_z = [(depth == 0, partner), (depth == 0, own_relay), (depth == 0, other_relay)]
    along_z += [(depth == 1, above), (depth == 1, below)]
    along_z += [(depth == 1, device(lax.rem(2 * y, 8), x, core)), (depth == 1, device(lax.rem(2 * y + 1, 8), x, core))]
    along_z += [(depth == 2, device(lax.rem(2 * y + jnp.where(upper, 3, 6), 8), x, core))]
    for condition, other in along_z:

        @pl.when(condition)
        def _(other=other):
            pl.semaphore_signal(barrier, inc=1, device_id={"blk": other}, device_id_type=MESH)

    for other in (right, left, sibling):
        pl.semaphore_signal(barrier, inc=1, device_id={"blk": other}, device_id_type=MESH)
    for step in (1, 2, 3):
        pl.semaphore_signal(
            barrier, inc=1, device_id={"head": lax.rem(y + step, 4)}, device_id_type=MESH
        )

    @pl.when(depth == 0)
    def _():
        for copy in own_copies:
            copy.start()

    for copy in small:
        copy.start()

    def remote(src, dst, sent, received, target):
        return pltpu.make_async_remote_copy(
            src_ref=src, dst_ref=dst, send_sem=send_sem.at[sent], recv_sem=recv_sem.at[received],
            device_id=target, device_id_type=MESH,
        )

    def block(index, cc, sent, received, target, half=None, meta=True, src=None):
        ref = keys.at[index, cc]
        if half is not None:
            ref = keys.at[index, cc, pl.ds(96 * half, 96)]
        copies = [remote(ref if src is None else src, ref, sent, received, {"blk": target})]
        if meta:
            ref = metas.at[index, cc]
            copies.append(remote(ref, ref, sent + META_OUT, received + META, {"blk": target}))
        return copies

    def sends(name):
        kind, phase, half = EVENTS[name]
        index = item(phase, kind)
        result = []
        step = 2 * phase + half
        meta = half == 0

        def add(condition, sent, received, target, at_end=True, src=None):
            result.append((condition, block(index, core, sent, received, target, half, meta, src), at_end))

        if kind == 0:
            if phase == 0:
                own = single_k.at[pl.ds(96 * half, 96)]
                add(depth == 0, Z_BACK + half, Z_IN + half, own_relay, False, own)
                add(depth == 0, Z_OUT + half, Z_IN + 2 + half, partner, True, own)
                add(depth == 0, RIGHT_OUT + step, LEFT_IN + step, right, True, own)
                add(depth == 0, LEFT_OUT + step, RIGHT_IN + step, left, True, own)
            add(depth == 1, Z_OUT + step, Z_IN + step, above)
            add(depth == 1, Z_BACK + step, Z_IN + step, below)
            passed = depth > 0 if phase == 0 else None
            add(passed, RIGHT_OUT + step, LEFT_IN + step, right)
            add(passed, LEFT_OUT + step, RIGHT_IN + step, left)
        if kind == 1 and half == 0:
            add(None, HALF_RIGHT_OUT + phase, HALF_LEFT_IN + phase, right)
        if kind == 2 and half == 1:
            add(None, HALF_LEFT_OUT + phase, HALF_RIGHT_IN + phase, left)
        if half == 1:
            i = chunk_of(phase, kind)
            result.append((None, block(index, core, CORE_OUT + i, CORE_IN + i, sibling), True))
        return result

    def near_copies(half):
        own = single_k.at[pl.ds(96 * half, 96)]
        return block(own_index, core, Z_BACK + half, Z_IN + half, own_relay, half, half == 0, own)

    def far_copies(half):
        own = single_k.at[pl.ds(96 * half, 96)]
        return block(own_index, core, Z_LAST + half, Z_IN + 2 + half, other_relay, half, half == 0, own)

    def run(condition, copies, verb):
        def act():
            for copy in copies:
                getattr(copy, verb)()

        if condition is None:
            act()
        else:
            pl.when(condition)(act)

    def event(name):
        kind, phase, half = EVENTS[name]
        index = item(phase, kind)
        step = 2 * phase + half
        if kind == 3:
            arriving = block(index, core, 0, HALF_LEFT_IN + phase, sibling, 0)
            arriving += block(index, core, 0, HALF_RIGHT_IN + phase, sibling, 1, False)
        else:
            place = (Z_IN, LEFT_IN, RIGHT_IN)[kind] + step
            arriving = block(index, core, 0, place, sibling, half, half == 0)
        run(depth > 0 if kind == 0 and phase == 0 else None, arriving, "wait_recv")
        for condition, copies, _ in sends(name):
            run(condition, copies, "start")

    slots = {
        name: jnp.where(depth == 0, when[0], jnp.where(depth == 1, when[1], when[2])) for name, when in SLOTS.items()
    }

    def events_at(step, names):
        for name in names:
            pl.when(slots[name] == step)(lambda name=name: event(name))

    pl.semaphore_wait(barrier, jnp.where(depth == 0, 9, jnp.where(depth == 1, 10, 7)))
    first = [copies for condition, copies, _ in sends("z0") if condition is not None][:4]

    @pl.when(depth == 0)
    def _():
        for copies in first:
            copies[0].start()
        for copy in own_copies[:3]:
            copy.wait()
        metas[own_index, core] = jnp.zeros((16, 256), F32)
        metas[own_index, core, :12, :192] = v_kframes[...]
        metas[own_index, core, 12:13, :192] = v_kchain[...].astype(F32)
        metas[own_index, core, 13:14, :192] = v_kmask[...].astype(F32)
        for copies in first:
            copies[1].start()

    for copy in pair_copies:
        copy.start()
    out_copy.start()

    for copy in small:
        copy.wait()
    scalar, compact = own_rows(
        v_single[...], v_frames[...], v_chain[...], v_wq[...], v_wk[...], v_wqp[...], head_weight, chain_bias
    )
    pack_rows[y, :, :384] = scalar
    pack_rows[y, :, 384:] = compact
    key_points, values, value_points = own_weights(v_wkp[...], v_wv[...], v_wvp[...])
    pack_weights[y, :48] = key_points
    pack_weights[y, 48:96] = values
    pack_weights[y, 96:] = value_points

    def exchange(src, dst, sent, received):
        out, arriving = [], []
        for step in (1, 2, 3):
            peer = lax.rem(y + step, 4)
            origin = lax.rem(y + 4 - step, 4)
            out.append(remote(src(peer), dst.at[y], sent + step - 1, received + step - 1, {"head": peer}))
            arriving.append(
                remote(dst.at[origin], dst.at[origin], sent + step - 1, received + step - 1, {"head": peer})
            )
        return out, arriving

    rows_sent, rows_arriving = exchange(lambda peer: pack_rows.at[y], pack_rows, ROWS_OUT, ROWS_IN)
    weights_sent, weights_arriving = exchange(
        lambda peer: pack_weights.at[y], pack_weights, WEIGHTS_OUT, WEIGHTS_IN
    )
    for copy in rows_sent + weights_sent:
        copy.start()

    row = iota((ROWS, 16), 0)
    frames = nt(ones_where(by12(row) == iota((ROWS, 16), 1), F32), v_frames[...], HIGH)
    centers[...] = frames[:, 9:12]
    lane = iota((1, 128), 1)
    axis = (lane - 16) >> 3
    inside = (lane >= 16) & (lane < 40)
    entry = iota((12, 128), 0)
    for b in range(3):
        turns[b] = mm(frames, ones_where((entry == 3 * b + axis) & inside, F32), HIGH)

    run(depth == 0, near_copies(0), "wait_send")
    run(depth == 0, far_copies(0), "start")

    col = iota((32, 12), 1)
    pick_row = iota((32, 12), 0)
    first = mm(ones_where(pick_row == col), v_wbias[...])
    second = mm(ones_where(pick_row == col + 12), v_wbias[...])
    bias_rows[:, :128] = first.astype(BF16)
    bias_rows[:, 128:] = second.astype(BF16)

    def bias_step(t, _):
        pltpu.make_async_copy(pair.at[pl.ds(2 * t, 2)], pairs.at[pl.ds(2 * t, 2)], pair_sem.at[t]).wait()
        for c in range(0, CHUNKS, 2):
            block_a = pairs[2 * t, c : c + 2].reshape(2 * KEYS, 128)
            block_b = pairs[2 * t + 1, c : c + 2].reshape(2 * KEYS, 128)
            out = nt(bias_rows[...], jnp.concatenate([block_a, block_b], axis=1))[:GROUP]
            out = short(out) * WEIGHT_L
            bias[c, t] = out[:, :KEYS]
            bias[c + 1, t] = out[:, KEYS:]
        run((depth == 0) & (t == 1), far_copies(0), "wait_send")
        run((depth == 0) & (t == 3), near_copies(1), "wait_send")
        run((depth == 0) & (t == 3), far_copies(1), "start")
        run((depth == 0) & (t == 1), own_copies[3:], "wait")
        events_at(t, [name for name, when in SLOTS.items() if any(0 <= k < 8 for k in when)])
        return 0

    lax.fori_loop(0, GROUPS, bias_step, 0)
    events_at(8, ["z2", "z3"])
    events_at(9, [name for name, when in SLOTS.items() if 9 in when])

    for copy in rows_arriving + weights_arriving:
        copy.wait_recv()
    for_single, for_other, factor = all_rows(pack_rows[...].reshape(ROWS, 512))
    projections[:ROWS] = for_single
    rows_other[...] = for_other
    factors[...] = -factor
    packs = pack_weights[...]
    row, col = iota((ROWS, ROWS), 0), iota((ROWS, ROWS), 1)
    place = row & 15
    pick = col == (place >> 2) * 48 + (row >> 6) * 16 + ((row >> 4) & 3) * 4 + (place & 3)
    projections[ROWS : 2 * ROWS] = mm(ones_where(pick), packs[:, :48].reshape(ROWS, 384)).astype(BF16)
    w_values[...] = packs[:, 48:96].reshape(ROWS, 384)
    row, col = iota((288, 320), 0), iota((288, 320), 1)
    b = by96(row)
    rest = row - b * 96
    owner = by24(rest)
    pick = col == owner * 80 + b * 24 + rest - owner * 24
    projections[2 * ROWS :] = mm(ones_where(pick), packs[:, 96:].reshape(320, 384)).astype(BF16)

    acc_pair[...] = jnp.zeros_like(acc_pair)
    acc_single[...] = jnp.zeros_like(acc_single)
    acc_points[...] = jnp.zeros_like(acc_points)
    top[...] = jnp.full_like(top, -1e30)
    total[...] = jnp.zeros_like(total)

    indices = [item(*pair) for pair in ((0, 0), (1, 0), (0, 1), (0, 2), (1, 1), (1, 2), (0, 3), (1, 3))]

    def index_of(i):
        value = indices[7]
        for k in range(7):
            value = jnp.where(i == k, indices[k], value)
        return value

    def key_meta(index):
        half = iota((16, 128), 1) < 64
        first, second = metas[index, 0], metas[index, 1]
        start = pltpu.roll(second[:, :128], 64, 1)
        end = pltpu.roll(second[:, 128:], 64, 1)
        return [first[:, :128], jnp.where(half, first[:, 128:], start), jnp.where(half, start, end)]

    def front(s):
        pair_of = [index_of(2 * s), index_of(2 * s + 1)]
        for k, index in enumerate(pair_of):
            i = 2 * s + k
            here = keys.at[index, 1 - core]
            remote(here, here, 0, CORE_IN + i, {"blk": sibling}).wait_recv()
            here = metas.at[index, 1 - core]
            remote(here, here, 0, META + CORE_IN + i, {"blk": sibling}).wait_recv()

        single = jnp.concatenate([keys[index].reshape(KEYS, 384) for index in pair_of], axis=0)
        meta = jnp.concatenate(key_meta(pair_of[0]) + key_meta(pair_of[1]), axis=1)

        def placed(local, rows):
            result = []
            for a in range(3):
                moved = meta[9 + a : 10 + a] + meta[3 * a : 3 * a + 1] * local[:rows]
                moved = moved + meta[3 * a + 1 : 3 * a + 2] * local[rows : 2 * rows]
                moved = moved + meta[3 * a + 2 : 3 * a + 3] * local[2 * rows :]
                result.append(moved.astype(BF16))
            return result

        projected = nt(projections[...], single)
        points = placed(projected[ROWS : 2 * ROWS], 64)
        square = 0.0
        for part in points:
            wide = part.astype(F32)
            square = square + wide * wide
        norm = square[:16] + square[16:32] + square[32:48] + square[48:]
        norms = [v.astype(BF16) for v in split3(norm * factors[...])]
        width = 2 * KEYS
        chains = ones_where(meta[12:13] == iota((32, width), 0).astype(F32))
        others = jnp.concatenate(
            points + points + [chains, chains] + norms + [jnp.full((16, width), 1.0, BF16)], axis=0
        )
        logit = projected[:ROWS] + mm(rows_other[...], others)
        logit = logit + jnp.concatenate([bias[index].reshape(ROWS, KEYS) for index in pair_of], axis=1)
        logit = jnp.where(meta[13:14] > 0.5, logit, -1000000000.0)
        vpoints = jnp.concatenate(placed(projected[2 * ROWS :], 96), axis=0)
        return logit, vpoints

    def back(s, logit, vpoints):
        pair_of = [index_of(2 * s), index_of(2 * s + 1)]
        single = jnp.concatenate([keys[index].reshape(KEYS, 384) for index in pair_of], axis=0)
        old = top[...]
        new = jnp.maximum(old, jnp.max(logit, axis=1, keepdims=True))
        scale = jnp.exp(old - new)
        weight = jnp.exp(logit - new)
        top[...] = new
        total[...] = total[...] * scale + jnp.sum(weight, axis=1, keepdims=True)
        weight_b = weight.astype(BF16)
        acc_single[...] = acc_single[...] * scale + mm(weight_b, single)
        acc_points[...] = acc_points[...] * scale + nt(weight_b, vpoints)
        upper_rows = iota((GROUP, 128), 0) < 12
        for g in range(GROUPS):
            lo = g * GROUP
            there = jnp.concatenate(
                [
                    jnp.concatenate([pairs[2 * g, index] for index in pair_of], axis=0),
                    jnp.concatenate([pairs[2 * g + 1, index] for index in pair_of], axis=0),
                ],
                axis=1,
            )
            out = mm(weight[lo : lo + GROUP].astype(BF16), there)
            out = jnp.where(upper_rows, out[:, :128], out[:, 128:])
            acc_pair[g] = acc_pair[g] * scale[lo : lo + GROUP] + out

    def key_step(s, before):
        events_at(s + 10, [name for name, when in SLOTS.items() if max(when) > 9])
        after = front(s)
        back(s - 1, *before)
        return after

    back(3, *lax.fori_loop(1, 4, key_step, front(0)))

    inverse = 1.0 / total[...]
    row = iota((ROWS, 1), 0)
    query = by12(row)
    head = row - query * 12
    part_in[y] = (acc_pair[...].reshape(ROWS, 128) * inverse).astype(BF16)
    parts_sent, parts_arriving = exchange(lambda peer: part_in.at[y], part_in, PART_OUT, PART_IN)
    for copy in parts_sent:
        copy.start()
    hi, lo = split2(acc_single[...] * inverse)
    scalar = nt(hi.astype(BF16), w_values[...]) + nt(lo.astype(BF16), w_values[...])
    scalar = jnp.where((iota((ROWS, ROWS), 1) >> 4) == head, scalar, 0.0).astype(BF16)
    lane = iota((1, 128), 1)
    again = lane & 63
    source = iota((ROWS, 128), 0)
    other = mm(scalar, ones_where(((source & 15) == again) & (again < 16)))
    center = centers[...]
    col = iota((1, 288), 1)
    axis = by96(col)
    center = jnp.where(axis == 0, center[:, :1], jnp.where(axis == 1, center[:, 1:2], center[:, 2:3]))
    shifted = jnp.where(((col - axis * 96) >> 3) == head, acc_points[...] * inverse - center, 0.0).astype(BF16)
    source = iota((288, 128), 0)
    other = other + mm(shifted, ones_where(again == by96(source) * 8 + (source & 7) + 16))
    for start, value in ((40, top[...]), (43, total[...])):
        for step, piece in enumerate(split3(value)):
            other = jnp.where(again == start + step, piece, other)
    half = ROWS // 2
    rest_in[y] = jnp.where(lane < 64, other[:half], other[half:]).astype(BF16)

    rest_sent, rest_arriving = exchange(lambda peer: rest_in.at[y], rest_in, REST_OUT, REST_IN)
    for copy in rest_sent:
        copy.start()
    for copy in parts_arriving + rest_arriving:
        copy.wait_recv()

    pair_parts = [part_in[k].astype(F32) for k in range(4)]
    others = []
    for k in range(4):
        both = rest_in[k].astype(F32)
        others.append(jnp.concatenate([both, pltpu.roll(both, 64, 1)], axis=0))
    tops = [p[:, 40:41] + p[:, 41:42] + p[:, 42:43] for p in others]
    best = jnp.maximum(jnp.maximum(tops[0], tops[1]), jnp.maximum(tops[2], tops[3]))
    shares = [
        (p[:, 43:44] + p[:, 44:45] + p[:, 45:46]) * jnp.exp(t - best) for p, t in zip(others, tops)
    ]
    inverse = 1.0 / (shares[0] + shares[1] + shares[2] + shares[3])
    shares = [share * inverse for share in shares]
    o_pair = sum(p * s for p, s in zip(pair_parts, shares)).astype(BF16)
    other = sum(p * s for p, s in zip(others, shares))
    inside = (lane >= 16) & (lane < 40)
    point = lane & 7
    source = iota((128, 128), 0)
    first, second = split2(other)
    located = 0.0
    for b in range(3):
        pick = ones_where((source == point + 16 + 8 * b) & inside)
        located = located + turns[b] * (mm(first.astype(BF16), pick) + mm(second.astype(BF16), pick))
    last = (lane >= 40) & (lane < 48)
    pick = (source >= 16) & (source < 40) & ((source & 7) == point) & last
    first, second = split2(located * located)
    pick = ones_where(pick)
    length = jnp.sqrt(mm(first.astype(BF16), pick) + mm(second.astype(BF16), pick) + 1e-08)
    feats = jnp.where(lane < 16, other, jnp.where(inside, located, jnp.where(last, length, 0.0)))
    feats = jnp.concatenate([o_pair, feats.astype(BF16)], axis=1)
    row, col = iota((ROWS, ROWS), 0), iota((ROWS, ROWS), 1)
    query = by12(col)
    pick = ones_where(((row & 15) == query) & ((row >> 4) == col - query * 12))
    feats = mm(pick, feats).astype(BF16)
    out_copy.wait()
    update = v_single[...].astype(F32)
    for k in range(HEADS):
        here = feats[16 * k : 16 * k + 16]
        w = 176 * k
        update = update + mm(here[:, :128], v_wout[w + 16 : w + 144])
        rest = jnp.concatenate([v_wout[w : w + 16], v_wout[w + 144 : w + 176]], axis=0)
        update = update + mm(here[:, 128:176], rest)
    mixed_out[...] = update

    for name in EVENTS:
        for condition, copies, at_end in sends(name):
            if at_end:
                run(condition, copies, "wait_send")
    run(depth == 0, far_copies(1), "wait_send")
    for copy in rows_sent + weights_sent + parts_sent + rest_sent:
        copy.wait_send()


def finish(mixed_ref, gain, w_frame, frames, single_out, frames_out):
    mixed = mixed_ref[...]
    mean = jnp.mean(mixed, axis=1, keepdims=True)
    centered = mixed - mean
    var = jnp.mean(centered * centered, axis=1, keepdims=True)
    out = (centered / jnp.sqrt(var + 1e-05) * gain[...][None]).astype(BF16)
    single_out[...] = out
    shift = nt(w_frame[...], out)
    u = [shift[k : k + 1] for k in range(6)]
    length = jnp.sqrt(1.0 + u[0] * u[0] + u[1] * u[1] + u[2] * u[2])
    turn = quat_rotation(1.0 / length, u[0] / length, u[1] / length, u[2] / length)
    rot = [frames[k : k + 1] for k in range(12)]
    for a in range(3):
        for c in range(3):
            k = 3 * a + c
            frames_out[k : k + 1] = (
                rot[3 * a] * turn[c] + rot[3 * a + 1] * turn[3 + c] + rot[3 * a + 2] * turn[6 + c]
            )
        moved = rot[3 * a] * u[3] + rot[3 * a + 1] * u[4] + rot[3 * a + 2] * u[5]
        frames_out[9 + a : 10 + a] = moved + rot[9 + a]


def per_device(
    query_single, query_frames, query_chain, key_single, key_frames, key_chain, key_mask, pair,
    w_q, w_k, w_v, w_qp, w_kp, w_vp, w_bias, head_weight, chain_bias, w_out, ln_gain, w_frame,
):
    pair = pair.reshape(16, CHUNKS, KEYS, 128)
    vm = pltpu.VMEM
    anywhere = pl.BlockSpec(memory_space=pl.ANY)
    scalars = pl.BlockSpec(memory_space=pltpu.SMEM)
    inside = pl.BlockSpec(memory_space=pltpu.VMEM)
    mixed = pl.pallas_call(
        kernel,
        out_shape=jax.ShapeDtypeStruct((16, 384), F32),
        in_specs=[anywhere] * 16 + [scalars] * 2,
        out_specs=inside,
        scratch_shapes=[
            vm((16, 384), BF16), vm((12, 16), F32), vm((1, 16), jnp.int32), vm((12, 192), F32),
            vm((1, 192), jnp.int32), vm((1, 192), jnp.int32), vm((48, 384), BF16), vm((48, 384), BF16),
            vm((48, 384), BF16), vm((36, 384), BF16), vm((36, 384), BF16), vm((72, 384), BF16),
            vm((12, 128), BF16), vm((2112, 384), BF16),
            vm((16, CHUNKS, KEYS, 128), BF16), vm((CHUNKS, 2, 192, 384), BF16), vm((CHUNKS, 2, 16, 256), F32),
            vm((CHUNKS, GROUPS, GROUP, KEYS), F32), vm((4, 48, 512), BF16), vm((4, 176, 384), BF16),
            vm((2 * ROWS + 288, 384), BF16), vm((ROWS, 512), BF16), vm((ROWS, 384), BF16), vm((16, 1), F32),
            vm((32, 256), BF16),
            vm((GROUPS, GROUP, 128), F32), vm((ROWS, 384), F32), vm((ROWS, 288), F32),
            vm((ROWS, 1), F32), vm((ROWS, 1), F32), vm((4, ROWS, 128), BF16), vm((4, ROWS // 2, 128), BF16),
            vm((ROWS, 3), F32), vm((3, ROWS, 128), F32),
            pltpu.SemaphoreType.DMA((15,)), pltpu.SemaphoreType.DMA((GROUPS,)),
            pltpu.SemaphoreType.DMA((80,)), pltpu.SemaphoreType.DMA((64,)),
        ],
        compiler_params=pltpu.CompilerParams(
            collective_id=0, has_side_effects=True, vmem_limit_bytes=56 * 1024 * 1024
        ),
    )(
        query_single, query_frames, query_chain[None], key_single, key_frames, key_chain[None], key_mask[None], pair,
        w_q.T, w_k.T, w_v.T, w_qp.T, w_kp.T, w_vp.T, w_bias.T, w_out, head_weight, chain_bias,
    )
    return pl.pallas_call(
        finish,
        out_shape=(jax.ShapeDtypeStruct((16, 384), BF16), jax.ShapeDtypeStruct((12, 16), F32)),
        in_specs=[inside] * 4,
        out_specs=(inside, inside),
    )(mixed, ln_gain, w_frame.T, query_frames)


def solution(mesh):
    rows = ("sample", "blk")
    heads = P(None, "head")
    in_specs = (
        P(rows, None), P(None, rows), P(rows), P(rows, None), P(None, rows), P(rows), P(rows),
        P(rows, "head", None), heads, heads, heads, heads, heads, heads, P(), P("head"), P("head"),
        P(), P(), P(),
    )
    out_specs = (P(rows, None), P(None, rows))
    return jax.shard_map(
        per_device, mesh=mesh, in_specs=in_specs, out_specs=out_specs, check_vma=False
    )
```
